32 devices in a mesh: pole: 2 (over y), row: 4 (over x, core), col: 4 (over z).
Axes of the slice: x: 2, y: 2, z: 4, core: 2. Of those that a mesh axis runs over, the one named last changes fastest.
Arguments:
- top_inverse: bfloat16 [8, 4, 4, 4, 256, 256], P('pole', 'row', None, 'col'), parts along dimension 0
- upper_factor: bfloat16 [8, 4, 8, 4, 256, 256], P('pole', 'row', None, 'col'), parts along dimension 0, may hold values from -0.109375 to 0.109375
- pivot_inverse: float32 [8, 4, 256, 256], P('pole', 'row'), parts along dimension 0
- widths: int32 [32], replicated, may hold values from 128 to 256
- order: int32 [16], replicated, may hold values from 0 to 15, as said below
- pattern: int32 [32, 16], replicated, may hold values from 0 to 1, as said below
Outputs:
- inverse_columns: bfloat16 [16, 4, 4, 4, 256, 256], P('pole', 'row', None, 'col'), parts along dimension 0
The draws below stay inside these ranges and needn't reach their ends.
There are 2 independent parts, one for each index of `pole`. The reference program is written for one: setup_inputs(seed, part) draws one part's arguments, and reference() takes and returns one part's arrays. A program takes and returns all parts, laid end to end along the dimension named above; an argument that names none is the same for every part. Nothing has to cross between parts.
Inputs may be any that keep to these rules, and one draw needn't show every extreme that they name: `order`: a permutation of the 16 window supernodes; positions p with equal p // 4 form one level of the elimination tree. pattern[J, K] is 1 only where J is an ancestor of K: a top supernode (J >= 16) or a window supernode of an earlier level in order; in particular 0 for J = K and for supernodes of the same level.
All inputs are finite; a program needn't handle non-finite values.
Results may differ from the reference program's by a relative error of at most 0.015.
Values may be sent and summed in bfloat16 or wider, within the bound.
No kernel may reach another device: no remote copies, remote signals or barrier semaphores. Data moves between devices by JAX's collectives and lax.ppermute only.
A program may use at most 128 MiB of HBM per device.

```python
import jax
import jax.numpy as jnp
from jax import lax

B = 256
SIB = 4
TOP = 16
NS = 16
NB = 32
N_ROW = 4
N_COL = 4


def level_order(key):
    return jax.random.permutation(key, NS).astype(jnp.int32)


def draw_order(key, part):
    sequence = level_order(key)
    return sequence


def draw_pattern(key, part):
    sequence = level_order(key)
    key = jax.random.fold_in(key, 5)
    position = jnp.zeros((NS,), jnp.int32).at[sequence].set(jnp.arange(NS, dtype=jnp.int32))
    depth = position // SIB
    row_depth = jnp.concatenate([depth, jnp.full((TOP,), -1, jnp.int32)])
    allowed = row_depth[:, None] < depth[None, :]
    coin = jax.random.randint(key, (NB, NS), 0, 10) < 7
    return (allowed & coin).astype(jnp.int32)


def draw_widths(key, part):
    key = jax.random.fold_in(key, 7)
    key_width, key_full = jax.random.split(key)
    drawn_sizes = jax.random.randint(key_width, (NB,), B // 2, B + 1)
    widest = jax.random.randint(key_full, (), 0, NB)
    return jnp.where(jnp.arange(NB) == widest, B, drawn_sizes).astype(jnp.int32)


def draw_top_inverse(key, part):
    key = jax.random.fold_in(key, 11)
    key_entries = jax.random.fold_in(key, 0)
    entries = jax.random.normal(key_entries, (TOP, TOP, B, B), jnp.float32)
    blocks = (entries + jnp.transpose(entries, (1, 0, 3, 2))) * 0.7071
    return blocks.reshape(TOP // N_ROW, N_ROW, TOP // N_COL, N_COL, B, B).astype(jnp.bfloat16)


def draw_pivot_inverse(key, part):
    key = jax.random.fold_in(key, 13)
    entries = jax.random.normal(key, (NS, B, B), jnp.float32)
    blocks = (entries + jnp.swapaxes(entries, 1, 2)) * 0.7071
    return blocks.reshape(NS // N_ROW, N_ROW, B, B).astype(jnp.float32)


def level_of(rng, dims, shards, smallest, largest):
    loudness, own = 1.0, jax.random.fold_in(rng, 6)
    for dim, blocks in shards:
        steps = jnp.exp(jax.random.uniform(jax.random.fold_in(own, dim), (blocks,), jnp.float32, smallest / len(shards), largest / len(shards)))
        loudness = loudness * jnp.repeat(steps, dims[dim] // blocks).reshape([-1 if axis == dim else 1 for axis in range(len(dims))])
    return loudness


def bell_draw(rng, extent, scale, most, cuts=(), kind=jnp.bfloat16):
    factor_of = level_of(rng, extent, cuts, -0.22, 0.18) if cuts else 1.0
    result = jax.random.normal(rng, extent, jnp.float32) * scale * factor_of
    return jnp.minimum(jnp.maximum(result, -most), most).astype(kind)


def setup_inputs(seed: int = 0, part: int = 0) -> dict:
    arg_keys = jax.random.split(jax.random.key(seed), 7)
    part_splits = jax.random.split(jax.random.fold_in(arg_keys[6], part), 7)
    return {
        "top_inverse": draw_top_inverse(jax.random.fold_in(jax.random.fold_in(arg_keys[6], part), 71), part),
        "upper_factor": bell_draw(part_splits[1], (NS // N_ROW, N_ROW, NB // N_COL, N_COL, B, B), (NB * B // 3) ** -0.5, 0.109375, ((1, 4), (3, 4))),
        "pivot_inverse": draw_pivot_inverse(jax.random.fold_in(jax.random.fold_in(arg_keys[6], part), 71), part),
        "widths": draw_widths(jax.random.fold_in(arg_keys[6], 71), part),
        "order": draw_order(jax.random.fold_in(arg_keys[6], 71), part),
        "pattern": draw_pattern(jax.random.fold_in(arg_keys[6], 71), part),
    }


def reference(top_inverse, upper_factor, pivot_inverse, widths, order, pattern):
    tile_size = top_inverse.shape[-1]
    window = order.shape[0]
    total_nodes = widths.shape[0]
    top_count = total_nodes - window
    top_blocks = top_inverse.reshape(top_count, top_count, tile_size, tile_size)
    factor = upper_factor.reshape(window, total_nodes, tile_size, tile_size)
    pivots = pivot_inverse.reshape(window, tile_size, tile_size)
    live_rows = (jnp.arange(tile_size)[None, :] < widths[:, None]).astype(jnp.bfloat16)
    held = jnp.zeros((total_nodes, total_nodes, tile_size, tile_size), jnp.bfloat16)
    held = held.at[window:, window:].set(top_blocks)
    zero_index = jnp.int32(0)

    def step(position, held):
        node_id = order[position].astype(jnp.int32)
        present = pattern[:, node_id].astype(jnp.bfloat16)
        panel = factor[node_id] * (present[:, None, None] * live_rows[:, None, :] * live_rows[node_id][None, :, None])
        grid = held.reshape(total_nodes, total_nodes // N_COL, N_COL, tile_size, tile_size).astype(jnp.float32)
        panel_grid = panel.reshape(total_nodes // N_COL, N_COL, tile_size, tile_size).astype(jnp.float32)
        parts = jnp.einsum("ibcpq,bcsq->icps", grid, panel_grid)
        rounded = lax.optimization_barrier(parts.astype(jnp.bfloat16))
        summed = jnp.sum(rounded.astype(jnp.float32), axis=1)
        column_mask = present[:, None, None] * live_rows[:, :, None] * live_rows[node_id][None, None, :]
        column_new = (-summed).astype(jnp.bfloat16) * column_mask
        held = lax.dynamic_update_slice(held, column_new[:, None], (zero_index, node_id, zero_index, zero_index))
        held = lax.dynamic_update_slice(held, jnp.swapaxes(column_new, 1, 2)[None], (node_id, zero_index, zero_index, zero_index))
        pivot_total = jnp.einsum("jsq,jqt->st", panel.astype(jnp.float32), column_new.astype(jnp.float32))
        corner_mask = live_rows[node_id][:, None].astype(jnp.float32) * live_rows[node_id][None, :].astype(jnp.float32)
        corner = ((pivots[node_id] - pivot_total) * corner_mask).astype(jnp.bfloat16)
        held = lax.dynamic_update_slice(held, corner[None, None], (node_id, node_id, zero_index, zero_index))
        return held

    held = lax.fori_loop(0, window, step, held)
    columns = held[:, :window]
    return columns.reshape(total_nodes // N_ROW, N_ROW, window // N_COL, N_COL, tile_size, tile_size)
```

```python
import functools

import jax
import jax.numpy as jnp
from jax import lax
from jax.experimental import pallas as pl
from jax.experimental.pallas import tpu as pltpu
from jax.sharding import PartitionSpec as P

SIB = 4


def from_root(x, axis, root):
    mine = lax.axis_index(axis) == root
    return lax.psum(jnp.where(mine, x, jnp.zeros_like(x)), axis)


def per_device(top_inverse, upper_factor, pivot_inverse, widths, order, pattern):
    row_count = lax.axis_size("row")
    col_count = lax.axis_size("col")
    row_rank = lax.axis_index("row")
    col_rank = lax.axis_index("col")
    tile_size = top_inverse.shape[-1]
    total_nodes = widths.shape[0]
    window = order.shape[0]
    row_blocks = total_nodes // row_count
    col_blocks = total_nodes // col_count
    row_span = row_count // col_count
    factor = upper_factor[:, 0, :, 0]
    pivots = pivot_inverse[:, 0]
    live_rows = (
        lax.broadcasted_iota(jnp.int32, (total_nodes, tile_size), 1) < widths[:, None]
    ).astype(jnp.bfloat16)
    row_nodes = jnp.arange(row_blocks, dtype=jnp.int32) * row_count + row_rank
    col_nodes = jnp.arange(col_blocks, dtype=jnp.int32) * col_count + col_rank
    blocks_held = jnp.zeros((row_blocks, col_blocks, tile_size, tile_size), jnp.bfloat16)
    blocks_held = blocks_held.at[window // row_count :, window // col_count :].set(
        top_inverse[:, 0, :, 0]
    )
    members = SIB

    def fetch(node_id):
        local_rows = lax.dynamic_index_in_dim(factor, node_id // row_count, 0, keepdims=False)
        return from_root(local_rows, "row", node_id % row_count)

    def panel(node_id):
        received = fetch(node_id)
        present = pattern[col_nodes, node_id].astype(jnp.bfloat16)
        keep_mask = (
            present[:, None, None]
            * live_rows[col_nodes][:, None, :]
            * live_rows[node_id][None, :, None]
        )
        return received * keep_mask

    def step(position, blocks_held):
        node_ids = lax.dynamic_slice_in_dim(order, position * members, members)
        node_list = [node_ids[member] for member in range(members)]
        panels = jnp.stack([panel(node_id) for node_id in node_list])
        partial_value = jnp.einsum(
            "abpq,ibsq->iaps", blocks_held, panels, preferred_element_type=jnp.float32
        )
        summed = lax.psum_scatter(
            partial_value.astype(jnp.bfloat16), "col", scatter_dimension=2, tiled=True
        ).astype(jnp.float32)
        row_share = (-summed).astype(jnp.bfloat16)
        column_new = lax.all_gather(row_share, "col", axis=2, tiled=True)
        present = jnp.transpose(pattern[row_nodes][:, node_ids]).astype(jnp.bfloat16)
        node_live = live_rows[node_ids]
        column_mask = (
            present[:, :, None, None]
            * live_rows[row_nodes][None, :, :, None]
            * node_live[:, None, None, :]
        )
        column_new = column_new * column_mask
        for member, node_id in enumerate(node_list):
            column_at = node_id // col_count
            current = lax.dynamic_slice_in_dim(blocks_held, column_at, 1, 1)
            update = jnp.where(
                col_rank == node_id % col_count, column_new[member][:, None], current
            )
            blocks_held = lax.dynamic_update_slice_in_dim(blocks_held, update, column_at, 1)
        arrived = []
        for offset in range(row_span):
            arrived.append(from_root(column_new, "row", col_rank + offset * col_count))
        mirror = jnp.stack(arrived, 2).reshape(members, row_blocks * row_span, tile_size, tile_size)
        pivot_part = jnp.einsum(
            "ibsq,ibqt->ist", panels, mirror, preferred_element_type=jnp.float32
        )
        pivot_total = lax.psum(pivot_part.astype(jnp.bfloat16), "col").astype(jnp.float32)
        for member, node_id in enumerate(node_list):
            row_at = node_id // row_count
            column_at = node_id // col_count
            on_row = row_rank == node_id % row_count
            on_col = col_rank == node_id % col_count
            current = lax.dynamic_slice_in_dim(blocks_held, row_at, 1, 0)
            flipped = jnp.swapaxes(mirror[member], 1, 2)[None]
            update = jnp.where(on_row, flipped, current)
            own_pivot = lax.dynamic_index_in_dim(pivots, row_at, 0, keepdims=False)
            corner_mask = node_live[member][:, None].astype(jnp.float32) * node_live[member][
                None, :
            ].astype(jnp.float32)
            corner = ((own_pivot - pivot_total[member]) * corner_mask).astype(jnp.bfloat16)
            update = update.at[0, column_at].set(
                jnp.where(on_row & on_col, corner, update[0, column_at])
            )
            blocks_held = lax.dynamic_update_slice_in_dim(blocks_held, update, row_at, 0)
        return blocks_held

    blocks_held = lax.fori_loop(0, window // members, step, blocks_held)
    return blocks_held[:, : window // col_count][:, None, :, None]


VMEM_BYTES = 50 * 1024 * 1024
ORD = 2


def dot_nt(a, b):
    return lax.dot_general(a, b, (((1,), (1,)), ((), ())), preferred_element_type=jnp.float32)


def dot_nn(a, b):
    return jnp.dot(a, b, preferred_element_type=jnp.float32)


class Facts:
    def __init__(self, sc, window, total):
        self.sc, self.window = sc, window
        self.pat_at = ORD + window
        self.wid_at = self.pat_at + window * total
        self.r, self.c = sc[0], sc[1]

    def node(self, level, member):
        return self.sc[ORD + level * SIB + member]

    def pat(self, row, col):
        return self.sc[self.pat_at + row * self.window + col]

    def width(self, node):
        return self.sc[self.wid_at + node]


def keep(x, rows, cols):
    at_row = lax.broadcasted_iota(jnp.int32, x.shape, 0)
    at_col = lax.broadcasted_iota(jnp.int32, x.shape, 1)
    return jnp.where((at_row < rows) & (at_col < cols), x, 0.0)


def call(body, dims, sc, inputs, outs, scratch=(), hbm=(), out_hbm=False, flops=0):
    specs = [pl.BlockSpec(memory_space=pltpu.SMEM)]
    for at in range(len(inputs)):
        specs.append(pl.BlockSpec(memory_space=pl.ANY if at in hbm else pltpu.VMEM))
    out_space = pl.ANY if out_hbm else pltpu.VMEM
    moved = sum(x.size * x.dtype.itemsize for x in list(inputs) + list(outs))

    def kernel(sc_ref, *refs):
        body(Facts(sc_ref, *dims), *refs)

    return pl.pallas_call(
        kernel,
        out_shape=list(outs),
        in_specs=specs,
        out_specs=[pl.BlockSpec(memory_space=out_space)] * len(outs),
        scratch_shapes=list(scratch),
        compiler_params=pltpu.CompilerParams(vmem_limit_bytes=VMEM_BYTES),
        cost_estimate=pl.CostEstimate(flops=flops, bytes_accessed=moved, transcendentals=0),
    )(sc, *inputs)


def swap(x, axis, d):
    count = lax.axis_size(axis)
    return lax.ppermute(x, axis, [(i, i ^ d) for i in range(count)])


def row_pieces(x):
    far = swap(x, "row", 2)
    return [x, swap(x, "row", 1), far, swap(far, "row", 1)]


def top_product(level, f, h, u0, u1, u2, u3, out, ubuf, lbuf, sems):
    pieces = (u0, u1, u2, u3)
    size = h.shape[-1]
    depth = h.shape[1]
    for m in range(SIB):
        node = f.node(level, m)
        for d in range(SIB):

            @pl.when((node % SIB) ^ f.r == d)
            def _():
                pltpu.make_async_copy(pieces[d].at[node // SIB], ubuf.at[m], sems.at[m]).start()

    for m in range(SIB):
        node = f.node(level, m)
        pltpu.make_async_copy(u0.at[0], ubuf.at[m], sems.at[m]).wait()
        for b in range(depth):
            at = f.window + b * SIB + f.c
            reach = jnp.where(f.pat(at, node) > 0, f.width(at), 0)
            kept = keep(ubuf[m, b].astype(jnp.float32), size, reach)
            lbuf[m, :, b * size : (b + 1) * size] = kept.astype(jnp.bfloat16)
    for a in range(h.shape[0]):
        rows = jnp.concatenate([h[a, b] for b in range(depth)], axis=1)
        for m in range(SIB):
            out[a, m] = dot_nt(rows, lbuf[m]).astype(jnp.bfloat16)


def own_blocks(levels, f, *refs):
    tops, wins, pivs = refs[0:4], refs[4:8], refs[8:12]
    by_slice, by_level, piv = refs[12:16], refs[16 : 15 + levels], refs[15 + levels]
    sems = refs[16 + levels]
    for wait in (False, True):
        for k in range(levels):
            node = f.node(k, f.r)
            at = node // SIB
            source = (node % SIB) ^ f.r
            for d in range(SIB):
                copies = [
                    pltpu.make_async_copy(tops[d].at[at, f.c ^ s], by_slice[s].at[k], sems.at[k, s])
                    for s in range(SIB)
                ]
                copies.append(pltpu.make_async_copy(pivs[d].at[at], piv.at[k], sems.at[k, SIB]))
                if k:
                    copies.append(
                        pltpu.make_async_copy(wins[d].at[at], by_level[k - 1], sems.at[k, SIB + 1])
                    )

                @pl.when(source == d)
                def _():
                    for copy in copies:
                        if wait:
                            copy.wait()
                        else:
                            copy.start()


def top_column(level, f, *refs):
    ys = refs[0:SIB]
    earlier = refs[SIB : SIB + SIB * level]
    out = refs[-1]
    node = f.node(level, f.r)
    acc = [y[...].astype(jnp.float32) for y in ys]
    if level:
        lw = refs[SIB + SIB * level]
        for j in range(level):
            for d in range(SIB):
                at = f.node(j, f.r ^ d)
                block = lw[at % SIB, at // SIB]
                block = jnp.where(f.pat(at, node) > 0, block, jnp.zeros_like(block))
                for e in range(SIB):
                    acc[e] += dot_nt(earlier[j * SIB + d][d ^ e], block)
    for e in range(SIB):
        row = f.window + f.c * SIB + (f.r ^ e)
        reach = jnp.where(f.pat(row, node) > 0, f.width(row), 0)
        out[e] = keep(-acc[e], reach, f.width(node)).astype(jnp.bfloat16)


def cross_product(level, levels, f, *refs):
    xs, ts, out = refs[0:4], refs[4:8], refs[8]
    turn = f.c ^ f.r
    for k in range(level, levels):
        node = f.node(k, f.r)
        parts = []
        for s in range(SIB):
            row = f.window + f.c * SIB + (f.c ^ s)
            block = ts[s][k]
            parts.append(jnp.where(f.pat(row, node) > 0, block, jnp.zeros_like(block)))
        left = jnp.concatenate(parts, axis=1)
        for d in range(SIB if k > level else 1):
            right = jnp.concatenate([xs[d][turn ^ (s ^ d)] for s in range(SIB)], axis=0)
            at = (k - level - 1) * SIB + d if k > level else (levels - 1 - level) * SIB
            out[at] = dot_nn(left, right).astype(jnp.bfloat16)


def window_column(k, f, *refs):
    vs, piv = refs[0 : k + 1], refs[k + 1]
    zs = refs[k + 2 : k + 2 + SIB * k]
    node = f.node(k, f.r)
    width = f.width(node)
    total = vs[k][vs[k].shape[0] - 1].astype(jnp.float32)
    if k:
        lw, out, ub = refs[-3], refs[-2], refs[-1]
        for i in range(k):
            for d in range(SIB):
                at = f.node(i, f.r ^ d)
                block = lw[at % SIB, at // SIB]
                ub[i * SIB + d] = jnp.where(f.pat(at, node) > 0, block, jnp.zeros_like(block))
        for j in range(k):
            for d in range(SIB):
                acc = vs[j][(k - j - 1) * SIB + d].astype(jnp.float32)
                for i in range(k):
                    for e in range(SIB):
                        left = ub[i * SIB + e]
                        if i > j:
                            acc += dot_nn(left, zs[i * SIB + e][j * SIB + (d ^ e)])
                        elif i < j:
                            acc += dot_nt(left, zs[j * SIB + d][i * SIB + (d ^ e)])
                        elif d == e:
                            acc += dot_nt(left, zs[j * SIB + d][j * SIB])
                at = f.node(j, f.r ^ d)
                reach = jnp.where(f.pat(at, node) > 0, f.width(at), 0)
                block = keep(-acc, width, reach).astype(jnp.bfloat16)
                out[j * SIB + d] = block
                total += dot_nt(ub[j * SIB + d], block)
    else:
        out = refs[-1]
    corner = piv[k].astype(jnp.float32) - total
    out[k * SIB] = keep(corner, width, width).astype(jnp.bfloat16)


def pack_rows(levels, f, *refs):
    xs, outs, sems = refs[: SIB * levels], refs[SIB * levels : SIB * levels + SIB], refs[-1]
    for wait in (False, True):
        for l in range(levels):
            for d in range(SIB):
                node = f.node(l, f.r ^ d)
                for s in range(SIB):

                    @pl.when((node % SIB) ^ f.c == s)
                    def _():
                        copy = pltpu.make_async_copy(
                            xs[l * SIB + d].at[d], outs[s].at[node // SIB], sems.at[l, d]
                        )
                        if wait:
                            copy.wait()
                        else:
                            copy.start()


def place(levels, f, *refs):
    rows, zs, out = refs[0:SIB], refs[SIB : SIB + SIB * levels], refs[-1]
    top = levels
    for s in range(SIB):
        out[top + (f.c ^ s)] = rows[s][...]
    out[0:top] = jnp.zeros_like(out[0:top])
    for k in range(levels):
        for d in range(SIB):
            z = zs[k * SIB + d]
            node = f.node(k, f.r ^ d)
            on_row, on_col = node % SIB == f.r, node % SIB == f.c
            if k:

                @pl.loop(0, k * SIB)
                def _(at):
                    other = f.node(at // SIB, f.r ^ d ^ (at % SIB))

                    @pl.when(on_row & (other % SIB == f.c))
                    def _():
                        out[node // SIB, other // SIB] = z[at]

                    @pl.when(on_col & (other % SIB == f.r))
                    def _():
                        out[other // SIB, node // SIB] = z[at].T

            @pl.when(on_row & on_col)
            def _():
                out[node // SIB, node // SIB] = z[k * SIB]


def square_plan(top_inverse, upper_factor, pivot_inverse, widths, order, pattern):
    row_rank = lax.axis_index("row")
    col_rank = lax.axis_index("col")
    size = top_inverse.shape[-1]
    total, window = widths.shape[0], order.shape[0]
    levels = window // SIB
    near = window // SIB
    bf16 = jnp.bfloat16
    dims = (window, total)

    def blocks(*lead, dtype=bf16):
        return jax.ShapeDtypeStruct((*lead, size, size), dtype)

    unit = 2 * size**3
    ranks = jnp.stack([row_rank, col_rank]).astype(jnp.int32)
    sc = jnp.concatenate([ranks, order, pattern.reshape(-1), widths])
    known = top_inverse[:, 0, :, 0]
    factor = upper_factor[:, 0, :, 0]
    tops = row_pieces(factor[:, near:])
    wins = row_pieces(factor[:, :near])
    pivs = row_pieces(pivot_inverse[:, 0].astype(bf16))

    sums = []
    for l in range(levels):
        (part,) = call(
            functools.partial(top_product, l),
            dims,
            sc,
            [known, *tops],
            [blocks(levels, SIB)],
            scratch=[
                pltpu.VMEM((SIB, levels, size, size), bf16),
                pltpu.VMEM((SIB, size, levels * size), bf16),
                pltpu.SemaphoreType.DMA((SIB,)),
            ],
            hbm=(1, 2, 3, 4),
            flops=64 * unit,
        )
        sums.append(lax.psum_scatter(part, "col", scatter_dimension=0, tiled=False))

    own = call(
        functools.partial(own_blocks, levels),
        dims,
        sc,
        [*tops, *wins, *pivs],
        [blocks(levels)] * SIB + [blocks(near)] * (levels - 1) + [blocks(levels)],
        scratch=[pltpu.SemaphoreType.DMA((levels, SIB + 2))],
        hbm=tuple(range(12)),
        out_hbm=True,
    )
    crossing = [own[0]] + [swap(own[s], "col", s) for s in range(1, SIB)]
    wide = [None] + [lax.all_gather(own[SIB + k], "col") for k in range(levels - 1)]
    pivot = own[SIB + levels - 1]

    columns, rights, solved = [], [], []
    for l in range(levels):
        ys = []
        for d in range(SIB):
            share = lax.dynamic_index_in_dim(sums[l], row_rank ^ d, 0, keepdims=False)
            ys.append(swap(share, "row", d) if d else share)
        inputs = ys + [x for xs in columns for x in xs] + ([wide[l]] if l else [])
        (column,) = call(
            functools.partial(top_column, l),
            dims,
            sc,
            inputs,
            [blocks(SIB)],
            flops=16 * l * unit,
        )
        columns.append(row_pieces(column))
        (right,) = call(
            functools.partial(cross_product, l, levels),
            dims,
            sc,
            [*columns[l], *crossing],
            [blocks(SIB * (levels - 1 - l) + 1)],
            flops=16 * (levels - l) * unit,
        )
        if rights:
            right, rights[-1] = lax.optimization_barrier((right, rights[-1]))
        rights.append(lax.psum(right, "col"))
        inputs = rights + [pivot] + [z for zs in solved for z in zs] + ([wide[l]] if l else [])
        (z,) = call(
            functools.partial(window_column, l),
            dims,
            sc,
            inputs,
            [blocks(SIB * l + 1)],
            scratch=[pltpu.VMEM((SIB * l, size, size), bf16)] if l else [],
            flops=(SIB * l * (SIB * l - 2) + 1) * unit,
        )
        solved.append(row_pieces(z))

    packed = call(
        functools.partial(pack_rows, levels),
        dims,
        sc,
        [x for xs in columns for x in xs],
        [blocks(levels)] * SIB,
        scratch=[pltpu.SemaphoreType.DMA((levels, SIB))],
        hbm=tuple(range(SIB * levels)),
        out_hbm=True,
    )
    rows = [packed[0]] + [swap(packed[s], "col", s) for s in range(1, SIB)]
    (out,) = call(
        functools.partial(place, levels),
        dims,
        sc,
        rows + [z for zs in solved for z in zs],
        [blocks(total // SIB, levels)],
    )
    return out[:, None, :, None]


def solution(mesh):
    in_specs = (
        P("pole", "row", None, "col", None, None),
        P("pole", "row", None, "col", None, None),
        P("pole", "row", None, None),
        P(),
        P(),
        P(),
    )
    out_specs = P("pole", "row", None, "col", None, None)
    square = mesh.shape["row"] == SIB and mesh.shape["col"] == SIB
    return jax.shard_map(
        square_plan if square else per_device, mesh=mesh, in_specs=in_specs, out_specs=out_specs, check_vma=False
    )
```

```python
import functools

import jax
import jax.numpy as jnp
from jax import lax
from jax.experimental import pallas as pl
from jax.experimental.pallas import tpu as pltpu
from jax.sharding import PartitionSpec as P

SIB = 4


def from_root(x, axis, root):
    mine = lax.axis_index(axis) == root
    return lax.psum(jnp.where(mine, x, jnp.zeros_like(x)), axis)


def per_device(top_inverse, upper_factor, pivot_inverse, widths, order, pattern):
    row_count = lax.axis_size("row")
    col_count = lax.axis_size("col")
    row_rank = lax.axis_index("row")
    col_rank = lax.axis_index("col")
    tile_size = top_inverse.shape[-1]
    total_nodes = widths.shape[0]
    window = order.shape[0]
    row_blocks = total_nodes // row_count
    col_blocks = total_nodes // col_count
    row_span = row_count // col_count
    factor = upper_factor[:, 0, :, 0]
    pivots = pivot_inverse[:, 0]
    live_rows = (
        lax.broadcasted_iota(jnp.int32, (total_nodes, tile_size), 1) < widths[:, None]
    ).astype(jnp.bfloat16)
    row_nodes = jnp.arange(row_blocks, dtype=jnp.int32) * row_count + row_rank
    col_nodes = jnp.arange(col_blocks, dtype=jnp.int32) * col_count + col_rank
    blocks_held = jnp.zeros((row_blocks, col_blocks, tile_size, tile_size), jnp.bfloat16)
    blocks_held = blocks_held.at[window // row_count :, window // col_count :].set(
        top_inverse[:, 0, :, 0]
    )
    members = SIB

    def fetch(node_id):
        local_rows = lax.dynamic_index_in_dim(factor, node_id // row_count, 0, keepdims=False)
        return from_root(local_rows, "row", node_id % row_count)

    def panel(node_id):
        received = fetch(node_id)
        present = pattern[col_nodes, node_id].astype(jnp.bfloat16)
        keep_mask = (
            present[:, None, None]
            * live_rows[col_nodes][:, None, :]
            * live_rows[node_id][None, :, None]
        )
        return received * keep_mask

    def step(position, blocks_held):
        node_ids = lax.dynamic_slice_in_dim(order, position * members, members)
        node_list = [node_ids[member] for member in range(members)]
        panels = jnp.stack([panel(node_id) for node_id in node_list])
        partial_value = jnp.einsum(
            "abpq,ibsq->iaps", blocks_held, panels, preferred_element_type=jnp.float32
        )
        summed = lax.psum_scatter(
            partial_value.astype(jnp.bfloat16), "col", scatter_dimension=2, tiled=True
        ).astype(jnp.float32)
        row_share = (-summed).astype(jnp.bfloat16)
        column_new = lax.all_gather(row_share, "col", axis=2, tiled=True)
        present = jnp.transpose(pattern[row_nodes][:, node_ids]).astype(jnp.bfloat16)
        node_live = live_rows[node_ids]
        column_mask = (
            present[:, :, None, None]
            * live_rows[row_nodes][None, :, :, None]
            * node_live[:, None, None, :]
        )
        column_new = column_new * column_mask
        for member, node_id in enumerate(node_list):
            column_at = node_id // col_count
            current = lax.dynamic_slice_in_dim(blocks_held, column_at, 1, 1)
            update = jnp.where(
                col_rank == node_id % col_count, column_new[member][:, None], current
            )
            blocks_held = lax.dynamic_update_slice_in_dim(blocks_held, update, column_at, 1)
        arrived = []
        for offset in range(row_span):
            arrived.append(from_root(column_new, "row", col_rank + offset * col_count))
        mirror = jnp.stack(arrived, 2).reshape(members, row_blocks * row_span, tile_size, tile_size)
        pivot_part = jnp.einsum(
            "ibsq,ibqt->ist", panels, mirror, preferred_element_type=jnp.float32
        )
        pivot_total = lax.psum(pivot_part.astype(jnp.bfloat16), "col").astype(jnp.float32)
        for member, node_id in enumerate(node_list):
            row_at = node_id // row_count
            column_at = node_id // col_count
            on_row = row_rank == node_id % row_count
            on_col = col_rank == node_id % col_count
            current = lax.dynamic_slice_in_dim(blocks_held, row_at, 1, 0)
            flipped = jnp.swapaxes(mirror[member], 1, 2)[None]
            update = jnp.where(on_row, flipped, current)
            own_pivot = lax.dynamic_index_in_dim(pivots, row_at, 0, keepdims=False)
            corner_mask = node_live[member][:, None].astype(jnp.float32) * node_live[member][
                None, :
            ].astype(jnp.float32)
            corner = ((own_pivot - pivot_total[member]) * corner_mask).astype(jnp.bfloat16)
            update = update.at[0, column_at].set(
                jnp.where(on_row & on_col, corner, update[0, column_at])
            )
            blocks_held = lax.dynamic_update_slice_in_dim(blocks_held, update, row_at, 0)
        return blocks_held

    blocks_held = lax.fori_loop(0, window // members, step, blocks_held)
    return blocks_held[:, : window // col_count][:, None, :, None]


VMEM_BYTES = 50 * 1024 * 1024
ORD = 2


def dot_nt(a, b):
    return lax.dot_general(a, b, (((1,), (1,)), ((), ())), preferred_element_type=jnp.float32)


def dot_nn(a, b):
    return jnp.dot(a, b, preferred_element_type=jnp.float32)


class Facts:
    def __init__(self, sc, window, total):
        self.sc, self.window = sc, window
        self.pat_at = ORD + window
        self.wid_at = self.pat_at + window * total
        self.r, self.c = sc[0], sc[1]

    def node(self, level, member):
        return self.sc[ORD + level * SIB + member]

    def pat(self, row, col):
        return self.sc[self.pat_at + row * self.window + col]

    def width(self, node):
        return self.sc[self.wid_at + node]


def keep(x, rows, cols):
    at_row = lax.broadcasted_iota(jnp.int32, x.shape, 0)
    at_col = lax.broadcasted_iota(jnp.int32, x.shape, 1)
    return jnp.where((at_row < rows) & (at_col < cols), x, 0.0)


def call(body, dims, sc, inputs, outs, scratch=(), hbm=(), flops=0):
    specs = [pl.BlockSpec(memory_space=pltpu.SMEM)]
    for at in range(len(inputs)):
        specs.append(pl.BlockSpec(memory_space=pl.ANY if at in hbm else pltpu.VMEM))
    moved = sum(x.size * x.dtype.itemsize for x in list(inputs) + list(outs))

    def kernel(sc_ref, *refs):
        body(Facts(sc_ref, *dims), *refs)

    return pl.pallas_call(
        kernel,
        out_shape=list(outs),
        in_specs=specs,
        out_specs=[pl.BlockSpec(memory_space=pltpu.VMEM)] * len(outs),
        scratch_shapes=list(scratch),
        compiler_params=pltpu.CompilerParams(vmem_limit_bytes=VMEM_BYTES),
        cost_estimate=pl.CostEstimate(flops=flops, bytes_accessed=moved, transcendentals=0),
    )(sc, *inputs)


def swap(x, axis, d):
    count = lax.axis_size(axis)
    return lax.ppermute(x, axis, [(i, i ^ d) for i in range(count)])


def row_pieces(x):
    far = swap(x, "row", 2)
    return [x, swap(x, "row", 1), far, swap(far, "row", 1)]


def col_pieces(x):
    far = swap(x, "col", 2)
    return [x, swap(x, "col", 1), far, swap(far, "col", 1)]


def col_sum(x):
    last = SIB - 1
    at_end = (lax.axis_index("col") == 0) | (lax.axis_index("col") == last)

    def add(a, b):
        return (a.astype(jnp.float32) + b.astype(jnp.float32)).astype(jnp.bfloat16)

    half = add(x, lax.ppermute(x, "col", [(0, 1), (last, last - 1)]))
    full = add(half, lax.ppermute(half, "col", [(1, 2), (2, 1)]))
    return jnp.where(at_end, lax.ppermute(full, "col", [(1, 0), (last - 1, last)]), full)


def top_product(level, f, h, u0, u1, u2, u3, out, ubuf, lbuf, sems):
    pieces = (u0, u1, u2, u3)
    size = h.shape[-1]
    depth = h.shape[1]
    for m in range(SIB):
        node = f.node(level, m)
        for d in range(SIB):

            @pl.when((node % SIB) ^ f.r == d)
            def _():
                pltpu.make_async_copy(pieces[d].at[node // SIB], ubuf.at[m], sems.at[m]).start()

    for m in range(SIB):
        node = f.node(level, m)
        pltpu.make_async_copy(u0.at[0], ubuf.at[m], sems.at[m]).wait()
        for b in range(depth):
            at = f.window + b * SIB + f.c
            reach = jnp.where(f.pat(at, node) > 0, f.width(at), 0)
            kept = keep(ubuf[m, b].astype(jnp.float32), size, reach)
            lbuf[m, :, b * size : (b + 1) * size] = kept.astype(jnp.bfloat16)
    for a in range(h.shape[0]):
        rows = jnp.concatenate([h[a, b] for b in range(depth)], axis=1)
        for m in range(SIB):
            out[a, m] = dot_nt(rows, lbuf[m]).astype(jnp.bfloat16)


def own_blocks(levels, f, *refs):
    tops, wins, pivs = refs[0:4], refs[4:8], refs[8:12]
    by_slice, by_level, piv = refs[12:16], refs[16 : 15 + levels], refs[15 + levels]
    sems = refs[16 + levels]
    for wait in (False, True):
        for k in range(levels):
            node = f.node(k, f.r)
            at = node // SIB
            source = (node % SIB) ^ f.r
            for d in range(SIB):
                copies = [
                    pltpu.make_async_copy(tops[d].at[at, f.c ^ s], by_slice[s].at[k], sems.at[k, s])
                    for s in range(SIB)
                ]
                copies.append(pltpu.make_async_copy(pivs[d].at[at], piv.at[k], sems.at[k, SIB]))
                if k:
                    copies.append(
                        pltpu.make_async_copy(wins[d].at[at], by_level[k - 1], sems.at[k, SIB + 1])
                    )

                @pl.when(source == d)
                def _():
                    for copy in copies:
                        if wait:
                            copy.wait()
                        else:
                            copy.start()


def top_column(level, f, *refs):
    ys = refs[0:SIB]
    earlier = refs[SIB : SIB + SIB * level]
    out = refs[-1]
    node = f.node(level, f.r)
    acc = [y[...].astype(jnp.float32) for y in ys]
    if level:
        lw = refs[-2]
        for j in range(level):
            for d in range(SIB):
                at = f.node(j, f.r ^ d)
                block = lw[(at % SIB) ^ f.c, at // SIB]
                block = jnp.where(f.pat(at, node) > 0, block, jnp.zeros_like(block))
                for e in range(SIB):
                    acc[e] += dot_nt(earlier[j * SIB + d][d ^ e], block)
    for e in range(SIB):
        row = f.window + f.c * SIB + (f.r ^ e)
        reach = jnp.where(f.pat(row, node) > 0, f.width(row), 0)
        out[e] = keep(-acc[e], reach, f.width(node)).astype(jnp.bfloat16)


def cross_product(level, levels, f, *refs):
    xs, ts, out = refs[0:4], refs[4:8], refs[8]
    turn = f.c ^ f.r
    for k in range(level + 1, levels):
        node = f.node(k, f.r)
        parts = []
        for s in range(SIB):
            row = f.window + f.c * SIB + (f.c ^ s)
            block = ts[s][k]
            parts.append(jnp.where(f.pat(row, node) > 0, block, jnp.zeros_like(block)))
        left = jnp.concatenate(parts, axis=1)
        for d in range(SIB):
            right = jnp.concatenate([xs[d][turn ^ (s ^ d)] for s in range(SIB)], axis=0)
            out[(k - level - 1) * SIB + d] = dot_nn(left, right).astype(jnp.bfloat16)


def pivot_product(level, f, x, t0, t1, t2, t3, out):
    turn = f.c ^ f.r
    left = jnp.concatenate([t[level] for t in (t0, t1, t2, t3)], axis=1)
    right = jnp.concatenate([x[turn ^ s] for s in range(SIB)], axis=0)
    out[0] = dot_nn(left, right).astype(jnp.bfloat16)


def window_column(k, f, *refs):
    vs, ds = refs[0:k], refs[k + SIB * (k - 1) : k + SIB * (2 * k - 1)]
    zs = [None] * SIB + list(refs[k : k + SIB * (k - 1)])
    lw, out, total_out, ub = refs[-4:]
    node = f.node(k, f.r)
    width = f.width(node)
    for i in range(k):
        for d in range(SIB):
            at = f.node(i, f.r ^ d)
            block = lw[(at % SIB) ^ f.c, at // SIB]
            ub[i * SIB + d] = jnp.where(f.pat(at, node) > 0, block, jnp.zeros_like(block))
    total = jnp.zeros(ub.shape[1:], jnp.float32)
    for j in range(k):
        for d in range(SIB):
            acc = vs[j][(k - j - 1) * SIB + d].astype(jnp.float32)
            for i in range(k):
                for e in range(SIB):
                    left = ub[i * SIB + e]
                    if i > j:
                        acc += dot_nn(left, zs[i * SIB + e][j * SIB + (d ^ e)])
                    elif i < j:
                        acc += dot_nt(left, zs[j * SIB + d][i * SIB + (d ^ e)])
                    elif d == e:
                        acc += dot_nt(left, ds[j * SIB + d][0])
            at = f.node(j, f.r ^ d)
            reach = jnp.where(f.pat(at, node) > 0, f.width(at), 0)
            block = keep(-acc, width, reach).astype(jnp.bfloat16)
            out[j * SIB + d] = block
            total += dot_nt(ub[j * SIB + d], block)
    total_out[0] = total


def pivot_block(k, f, piv, top_sum, *refs):
    out = refs[-1]
    total = top_sum[0].astype(jnp.float32)
    if k:
        total += refs[0][0]
    width = f.width(f.node(k, f.r))
    out[0] = keep(piv[k].astype(jnp.float32) - total, width, width).astype(jnp.bfloat16)


def pack_rows(levels, f, *refs):
    xs, outs, sems = refs[: SIB * levels], refs[SIB * levels : SIB * levels + SIB], refs[-1]
    for wait in (False, True):
        for l in range(levels):
            for d in range(SIB):
                node = f.node(l, f.r ^ d)
                for s in range(SIB):

                    @pl.when((node % SIB) ^ f.c == s)
                    def _():
                        copy = pltpu.make_async_copy(
                            xs[l * SIB + d].at[d], outs[s].at[node // SIB], sems.at[l, d]
                        )
                        if wait:
                            copy.wait()
                        else:
                            copy.start()


def place(levels, f, *refs):
    rows, out = refs[0:SIB], refs[-1]
    zs, ds = [None] * SIB + list(refs[SIB : SIB * levels]), refs[SIB * levels : SIB * 2 * levels]
    top = levels
    for s in range(SIB):
        out[top + (f.c ^ s)] = rows[s][...]
    out[0:top] = jnp.zeros_like(out[0:top])
    for k in range(levels):
        for d in range(SIB):
            z = zs[k * SIB + d]
            node = f.node(k, f.r ^ d)
            on_row, on_col = node % SIB == f.r, node % SIB == f.c
            if k:

                @pl.loop(0, k * SIB)
                def _(at):
                    other = f.node(at // SIB, f.r ^ d ^ (at % SIB))

                    @pl.when(on_row & (other % SIB == f.c))
                    def _():
                        out[node // SIB, other // SIB] = z[at]

                    @pl.when(on_col & (other % SIB == f.r))
                    def _():
                        out[other // SIB, node // SIB] = z[at].T

            @pl.when(on_row & on_col)
            def _():
                out[node // SIB, node // SIB] = ds[k * SIB + d][0]


def square_plan(top_inverse, upper_factor, pivot_inverse, widths, order, pattern):
    row_rank = lax.axis_index("row")
    col_rank = lax.axis_index("col")
    size = top_inverse.shape[-1]
    total, window = widths.shape[0], order.shape[0]
    levels = window // SIB
    near = window // SIB
    bf16 = jnp.bfloat16
    dims = (window, total)

    def blocks(*lead, dtype=bf16):
        return jax.ShapeDtypeStruct((*lead, size, size), dtype)

    unit = 2 * size**3
    ranks = jnp.stack([row_rank, col_rank]).astype(jnp.int32)
    sc = jnp.concatenate([ranks, order, pattern.reshape(-1), widths])
    known = top_inverse[:, 0, :, 0]
    factor = upper_factor[:, 0, :, 0]
    tops = row_pieces(factor[:, near:])
    wins = row_pieces(factor[:, :near])
    pivs = row_pieces(pivot_inverse[:, 0].astype(bf16))

    parts = [
        call(
            functools.partial(top_product, l),
            dims,
            sc,
            [known, *tops],
            [blocks(levels, SIB)],
            scratch=[
                pltpu.VMEM((SIB, levels, size, size), bf16),
                pltpu.VMEM((SIB, size, levels * size), bf16),
                pltpu.SemaphoreType.DMA((SIB,)),
            ],
            hbm=(1, 2, 3, 4),
            flops=64 * unit,
        )[0]
        for l in range(levels)
    ]
    sums = []
    for l in range(levels):
        sums.append(lax.psum_scatter(parts[l], "col", scatter_dimension=0, tiled=False))
        if l + 1 < levels:
            sums[l], *parts[l + 1 :] = lax.optimization_barrier((sums[l], *parts[l + 1 :]))

    own = call(
        functools.partial(own_blocks, levels),
        dims,
        sc,
        [*tops, *wins, *pivs],
        [blocks(levels)] * SIB + [blocks(near)] * (levels - 1) + [blocks(levels)],
        scratch=[pltpu.SemaphoreType.DMA((levels, SIB + 2))],
        hbm=tuple(range(12)),
    )
    crossing = [own[0]] + [swap(own[s], "col", s) for s in range(1, SIB)]
    wide = [None] + [jnp.stack(col_pieces(own[SIB + k])) for k in range(levels - 1)]
    pivot = own[SIB + levels - 1]

    columns, rights, solved, corners = [], [], [], []

    def flat(lists):
        return [x for xs in lists for x in xs]

    for l in range(levels):
        ys = []
        for d in range(SIB):
            share = lax.dynamic_index_in_dim(sums[l], row_rank ^ d, 0, keepdims=False)
            ys.append(swap(share, "row", d) if d else share)
        (column,) = call(
            functools.partial(top_column, l),
            dims,
            sc,
            ys + flat(columns) + ([wide[l]] if l else []),
            [blocks(SIB)],
            flops=16 * l * unit,
        )
        columns.append(row_pieces(column))
        (top_sum,) = call(
            functools.partial(pivot_product, l), dims, sc, [column, *crossing], [blocks(1)], flops=4 * unit
        )
        top_sum = col_sum(top_sum)
        if l + 1 < levels:
            (right,) = call(
                functools.partial(cross_product, l, levels),
                dims,
                sc,
                [*columns[l], *crossing],
                [blocks(SIB * (levels - 1 - l))],
                flops=16 * (levels - 1 - l) * unit,
            )
            rights.append(col_sum(right))
        inputs = [pivot, top_sum]
        if l:
            z, total_part = call(
                functools.partial(window_column, l),
                dims,
                sc,
                rights[:l] + flat(solved[1:]) + flat(corners) + [wide[l]],
                [blocks(SIB * l), blocks(1, dtype=jnp.float32)],
                scratch=[pltpu.VMEM((SIB * l, size, size), bf16)],
                flops=SIB * l * (SIB * l - 2) * unit,
            )
            inputs.append(total_part)
            solved.append(row_pieces(z))
        else:
            solved.append(None)
        (corner,) = call(functools.partial(pivot_block, l), dims, sc, inputs, [blocks(1)])
        corners.append([swap(corner, "row", d) if d else corner for d in range(SIB)])

    packed = call(
        functools.partial(pack_rows, levels),
        dims,
        sc,
        flat(columns),
        [blocks(levels)] * SIB,
        scratch=[pltpu.SemaphoreType.DMA((levels, SIB))],
        hbm=tuple(range(SIB * levels)),
    )
    rows = [packed[0]] + [swap(packed[s], "col", s) for s in range(1, SIB)]
    (out,) = call(
        functools.partial(place, levels),
        dims,
        sc,
        rows + flat(solved[1:]) + flat(corners),
        [blocks(total // SIB, levels)],
    )
    return out[:, None, :, None]


def solution(mesh):
    in_specs = (
        P("pole", "row", None, "col", None, None),
        P("pole", "row", None, "col", None, None),
        P("pole", "row", None, None),
        P(),
        P(),
        P(),
    )
    out_specs = P("pole", "row", None, "col", None, None)
    square = mesh.shape["row"] == SIB and mesh.shape["col"] == SIB
    return jax.shard_map(
        square_plan if square else per_device, mesh=mesh, in_specs=in_specs, out_specs=out_specs, check_vma=False
    )
```

```python
import functools

import jax
import jax.numpy as jnp
from jax import lax
from jax.experimental import pallas as pl
from jax.experimental.pallas import tpu as pltpu
from jax.sharding import PartitionSpec as P

SIB = 4


def from_root(x, axis, root):
    mine = lax.axis_index(axis) == root
    return lax.psum(jnp.where(mine, x, jnp.zeros_like(x)), axis)


def per_device(top_inverse, upper_factor, pivot_inverse, widths, order, pattern):
    row_count = lax.axis_size("row")
    col_count = lax.axis_size("col")
    row_rank = lax.axis_index("row")
    col_rank = lax.axis_index("col")
    tile_size = top_inverse.shape[-1]
    total_nodes = widths.shape[0]
    window = order.shape[0]
    row_blocks = total_nodes // row_count
    col_blocks = total_nodes // col_count
    row_span = row_count // col_count
    factor = upper_factor[:, 0, :, 0]
    pivots = pivot_inverse[:, 0]
    live_rows = (
        lax.broadcasted_iota(jnp.int32, (total_nodes, tile_size), 1) < widths[:, None]
    ).astype(jnp.bfloat16)
    row_nodes = jnp.arange(row_blocks, dtype=jnp.int32) * row_count + row_rank
    col_nodes = jnp.arange(col_blocks, dtype=jnp.int32) * col_count + col_rank
    blocks_held = jnp.zeros((row_blocks, col_blocks, tile_size, tile_size), jnp.bfloat16)
    blocks_held = blocks_held.at[window // row_count :, window // col_count :].set(
        top_inverse[:, 0, :, 0]
    )
    members = SIB

    def fetch(node_id):
        local_rows = lax.dynamic_index_in_dim(factor, node_id // row_count, 0, keepdims=False)
        return from_root(local_rows, "row", node_id % row_count)

    def panel(node_id):
        received = fetch(node_id)
        present = pattern[col_nodes, node_id].astype(jnp.bfloat16)
        keep_mask = (
            present[:, None, None]
            * live_rows[col_nodes][:, None, :]
            * live_rows[node_id][None, :, None]
        )
        return received * keep_mask

    def step(position, blocks_held):
        node_ids = lax.dynamic_slice_in_dim(order, position * members, members)
        node_list = [node_ids[member] for member in range(members)]
        panels = jnp.stack([panel(node_id) for node_id in node_list])
        partial_value = jnp.einsum(
            "abpq,ibsq->iaps", blocks_held, panels, preferred_element_type=jnp.float32
        )
        summed = lax.psum_scatter(
            partial_value.astype(jnp.bfloat16), "col", scatter_dimension=2, tiled=True
        ).astype(jnp.float32)
        row_share = (-summed).astype(jnp.bfloat16)
        column_new = lax.all_gather(row_share, "col", axis=2, tiled=True)
        present = jnp.transpose(pattern[row_nodes][:, node_ids]).astype(jnp.bfloat16)
        node_live = live_rows[node_ids]
        column_mask = (
            present[:, :, None, None]
            * live_rows[row_nodes][None, :, :, None]
            * node_live[:, None, None, :]
        )
        column_new = column_new * column_mask
        for member, node_id in enumerate(node_list):
            column_at = node_id // col_count
            current = lax.dynamic_slice_in_dim(blocks_held, column_at, 1, 1)
            update = jnp.where(
                col_rank == node_id % col_count, column_new[member][:, None], current
            )
            blocks_held = lax.dynamic_update_slice_in_dim(blocks_held, update, column_at, 1)
        arrived = []
        for offset in range(row_span):
            arrived.append(from_root(column_new, "row", col_rank + offset * col_count))
        mirror = jnp.stack(arrived, 2).reshape(members, row_blocks * row_span, tile_size, tile_size)
        pivot_part = jnp.einsum(
            "ibsq,ibqt->ist", panels, mirror, preferred_element_type=jnp.float32
        )
        pivot_total = lax.psum(pivot_part.astype(jnp.bfloat16), "col").astype(jnp.float32)
        for member, node_id in enumerate(node_list):
            row_at = node_id // row_count
            column_at = node_id // col_count
            on_row = row_rank == node_id % row_count
            on_col = col_rank == node_id % col_count
            current = lax.dynamic_slice_in_dim(blocks_held, row_at, 1, 0)
            flipped = jnp.swapaxes(mirror[member], 1, 2)[None]
            update = jnp.where(on_row, flipped, current)
            own_pivot = lax.dynamic_index_in_dim(pivots, row_at, 0, keepdims=False)
            corner_mask = node_live[member][:, None].astype(jnp.float32) * node_live[member][
                None, :
            ].astype(jnp.float32)
            corner = ((own_pivot - pivot_total[member]) * corner_mask).astype(jnp.bfloat16)
            update = update.at[0, column_at].set(
                jnp.where(on_row & on_col, corner, update[0, column_at])
            )
            blocks_held = lax.dynamic_update_slice_in_dim(blocks_held, update, row_at, 0)
        return blocks_held

    blocks_held = lax.fori_loop(0, window // members, step, blocks_held)
    return blocks_held[:, : window // col_count][:, None, :, None]


VMEM_BYTES = 50 * 1024 * 1024
ORD = 2


def dot_nt(a, b):
    return lax.dot_general(a, b, (((1,), (1,)), ((), ())), preferred_element_type=jnp.float32)


def dot_nn(a, b):
    return jnp.dot(a, b, preferred_element_type=jnp.float32)


class Facts:
    def __init__(self, sc, window, total):
        self.sc, self.window = sc, window
        self.pat_at = ORD + window
        self.wid_at = self.pat_at + window * total
        self.r, self.c = sc[0], sc[1]

    def node(self, level, member):
        return self.sc[ORD + level * SIB + member]

    def pat(self, row, col):
        return self.sc[self.pat_at + row * self.window + col]

    def width(self, node):
        return self.sc[self.wid_at + node]


def keep(x, rows, cols):
    at_row = lax.broadcasted_iota(jnp.int32, x.shape, 0)
    at_col = lax.broadcasted_iota(jnp.int32, x.shape, 1)
    return jnp.where((at_row < rows) & (at_col < cols), x, 0.0)


def call(body, dims, sc, inputs, outs, scratch=(), hbm=(), flops=0):
    specs = [pl.BlockSpec(memory_space=pltpu.SMEM)]
    for at in range(len(inputs)):
        specs.append(pl.BlockSpec(memory_space=pl.ANY if at in hbm else pltpu.VMEM))
    moved = sum(x.size * x.dtype.itemsize for x in list(inputs) + list(outs))

    def kernel(sc_ref, *refs):
        body(Facts(sc_ref, *dims), *refs)

    return pl.pallas_call(
        kernel,
        out_shape=list(outs),
        in_specs=specs,
        out_specs=[pl.BlockSpec(memory_space=pltpu.VMEM)] * len(outs),
        scratch_shapes=list(scratch),
        compiler_params=pltpu.CompilerParams(vmem_limit_bytes=VMEM_BYTES),
        cost_estimate=pl.CostEstimate(flops=flops, bytes_accessed=moved, transcendentals=0),
    )(sc, *inputs)


def swap(x, axis, d):
    count = lax.axis_size(axis)
    return lax.ppermute(x, axis, [(i, i ^ d) for i in range(count)])


def row_pieces(x):
    far = swap(x, "row", 2)
    return [x, swap(x, "row", 1), far, swap(far, "row", 1)]


def col_pieces(x):
    rank = lax.axis_index("col")
    last = SIB - 1
    up, down = [x], [x]
    for hop in range(1, SIB):
        down.append(lax.ppermute(down[-1], "col", [(i + 1, i) for i in range(SIB - hop)]))
        up.append(lax.ppermute(up[-1], "col", [(i, i + 1) for i in range(hop - 1, last)]))
    one = jnp.where(rank % 2 == 0, down[1], up[1])
    two = jnp.where(rank < 2, down[2], up[2])
    lower = jnp.where(rank == 0, down[3], down[1])
    upper = jnp.where(rank == last, up[3], up[1])
    return jnp.stack([x, one, two, jnp.where(rank < 2, lower, upper)])


def col_sum(x):
    last = SIB - 1
    at_end = (lax.axis_index("col") == 0) | (lax.axis_index("col") == last)

    def add(a, b):
        return (a.astype(jnp.float32) + b.astype(jnp.float32)).astype(jnp.bfloat16)

    half = add(x, lax.ppermute(x, "col", [(0, 1), (last, last - 1)]))
    full = add(half, lax.ppermute(half, "col", [(1, 2), (2, 1)]))
    return jnp.where(at_end, lax.ppermute(full, "col", [(1, 0), (last - 1, last)]), full)


def top_product(first, f, h, u0, u1, u2, u3, out, ubuf, lbuf, sems):
    pieces = (u0, u1, u2, u3)
    size = h.shape[-1]
    depth = h.shape[1]
    count = out.shape[1]
    for m in range(count):
        node = f.node(first, m)
        for d in range(SIB):

            @pl.when((node % SIB) ^ f.r == d)
            def _():
                pltpu.make_async_copy(pieces[d].at[node // SIB], ubuf.at[m], sems.at[m]).start()

    for m in range(count):
        node = f.node(first, m)
        pltpu.make_async_copy(u0.at[0], ubuf.at[m], sems.at[m]).wait()
        for b in range(depth):
            at = f.window + b * SIB + f.c
            reach = jnp.where(f.pat(at, node) > 0, f.width(at), 0)
            kept = keep(ubuf[m, b].astype(jnp.float32), size, reach)
            lbuf[m, :, b * size : (b + 1) * size] = kept.astype(jnp.bfloat16)
    for a in range(h.shape[0]):
        rows = jnp.concatenate([h[a, b] for b in range(depth)], axis=1)
        for m in range(count):
            out[a, m] = dot_nt(rows, lbuf[m]).astype(jnp.bfloat16)


def own_blocks(levels, f, *refs):
    tops, wins = refs[0:4], refs[4:8]
    by_slice, by_level = refs[8:12], refs[12 : 11 + levels]
    sems = refs[11 + levels]
    for wait in (False, True):
        for k in range(levels):
            node = f.node(k, f.r)
            at = node // SIB
            source = (node % SIB) ^ f.r
            for d in range(SIB):
                copies = [
                    pltpu.make_async_copy(tops[d].at[at, f.c ^ s], by_slice[s].at[k], sems.at[k, s])
                    for s in range(SIB)
                ]
                if k:
                    copies.append(
                        pltpu.make_async_copy(wins[d].at[at], by_level[k - 1], sems.at[k, SIB])
                    )

                @pl.when(source == d)
                def _():
                    for copy in copies:
                        if wait:
                            copy.wait()
                        else:
                            copy.start()


def own_pivots(levels, f, p0, p1, p2, p3, out):
    pieces = (p0, p1, p2, p3)
    for k in range(levels):
        node = f.node(k, f.r)
        for d in range(SIB):

            @pl.when((node % SIB) ^ f.r == d)
            def _():
                out[k] = pieces[d][node // SIB]


def top_column(level, f, *refs):
    ys = refs[0:SIB]
    earlier = refs[SIB : SIB + SIB * level]
    out = refs[-1]
    node = f.node(level, f.r)
    acc = [y[...].astype(jnp.float32) for y in ys]
    if level:
        lw = refs[-2]
        for j in range(level):
            for d in range(SIB):
                at = f.node(j, f.r ^ d)
                block = lw[(at % SIB) ^ f.c, at // SIB]
                block = jnp.where(f.pat(at, node) > 0, block, jnp.zeros_like(block))
                for e in range(SIB):
                    acc[e] += dot_nt(earlier[j * SIB + d][d ^ e], block)
    for e in range(SIB):
        row = f.window + f.c * SIB + (f.r ^ e)
        reach = jnp.where(f.pat(row, node) > 0, f.width(row), 0)
        out[e] = keep(-acc[e], reach, f.width(node)).astype(jnp.bfloat16)


def cross_product(level, levels, f, *refs):
    xs, ts, out = refs[0:4], refs[4:8], refs[8]
    turn = f.c ^ f.r
    for k in range(level, levels):
        node = f.node(k, f.r)
        parts = []
        for s in range(SIB):
            row = f.window + f.c * SIB + (f.c ^ s)
            block = ts[s][k]
            parts.append(jnp.where(f.pat(row, node) > 0, block, jnp.zeros_like(block)))
        left = jnp.concatenate(parts, axis=1)
        for d in range(SIB if k > level else 1):
            right = jnp.concatenate([xs[d][turn ^ (s ^ d)] for s in range(SIB)], axis=0)
            at = (k - level - 1) * SIB + d if k > level else (levels - 1 - level) * SIB
            out[at] = dot_nn(left, right).astype(jnp.bfloat16)


def window_column(k, low, high, f, *refs):
    whole = low == 0 and high == k
    count = high - low + whole
    vs = refs[0:count]
    zs = [refs[count + SIB * i : count + SIB * (i + 1)] for i in range(k)]
    at = count + SIB * k
    node = f.node(k, f.r)
    width = f.width(node)
    if k:
        lw, ub = refs[at], refs[-1]
        at += 1
    if whole:
        piv, out = refs[at], refs[at + 1]
        total = vs[-1][vs[-1].shape[0] - 1].astype(jnp.float32)
    else:
        out, share = refs[at], refs[at + 1]
        total = jnp.zeros(ub.shape[1:], jnp.float32)
    for i in range(k):
        for d in range(SIB):
            at = f.node(i, f.r ^ d)
            block = lw[(at % SIB) ^ f.c, at // SIB]
            ub[i * SIB + d] = jnp.where(f.pat(at, node) > 0, block, jnp.zeros_like(block))
    for j in range(low, high):
        for d in range(SIB):
            acc = vs[j - low][(k - j - 1) * SIB + d].astype(jnp.float32)
            for i in range(k):
                for e in range(SIB):
                    left = ub[i * SIB + e]
                    if i > j:
                        acc += dot_nn(left, zs[i][e][j * SIB + (d ^ e)])
                    elif i < j:
                        acc += dot_nt(left, zs[j][d][i * SIB + (d ^ e)])
                    elif d == e:
                        acc += dot_nt(left, zs[j][d][j * SIB])
            at = f.node(j, f.r ^ d)
            reach = jnp.where(f.pat(at, node) > 0, f.width(at), 0)
            block = keep(-acc, width, reach).astype(jnp.bfloat16)
            out[(j - low) * SIB + d] = block
            total += dot_nt(ub[j * SIB + d], block)
    if whole:
        corner = piv[k].astype(jnp.float32) - total
        out[k * SIB] = keep(corner, width, width).astype(jnp.bfloat16)
    else:
        share[0] = total


def pivot_block(k, f, piv, top_sum, *refs):
    out = refs[-1]
    total = top_sum[0].astype(jnp.float32)
    for part in refs[:-1]:
        total += part[0]
    width = f.width(f.node(k, f.r))
    out[0] = keep(piv[k].astype(jnp.float32) - total, width, width).astype(jnp.bfloat16)


def pack_rows(levels, f, *refs):
    xs, outs, sems = refs[: SIB * levels], refs[SIB * levels : SIB * levels + SIB], refs[-1]
    for wait in (False, True):
        for l in range(levels):
            for d in range(SIB):
                node = f.node(l, f.r ^ d)
                for s in range(SIB):

                    @pl.when((node % SIB) ^ f.c == s)
                    def _():
                        copy = pltpu.make_async_copy(
                            xs[l * SIB + d].at[d], outs[s].at[node // SIB], sems.at[l, d]
                        )
                        if wait:
                            copy.wait()
                        else:
                            copy.start()


def place(starts, f, *refs):
    rows, out = refs[0:SIB], refs[-1]
    top = out.shape[0] // 2
    for s in range(SIB):
        out[top + (f.c ^ s)] = rows[s][...]
    out[0:top] = jnp.zeros_like(out[0:top])
    for at, (k, low, count, corner) in enumerate(starts):
        for d in range(SIB):
            z = refs[SIB + at * SIB + d]
            node = f.node(k, f.r ^ d)
            on_row, on_col = node % SIB == f.r, node % SIB == f.c
            if count:

                @pl.loop(0, count)
                def _(at):
                    other = f.node(low + at // SIB, f.r ^ d ^ (at % SIB))

                    @pl.when(on_row & (other % SIB == f.c))
                    def _():
                        out[node // SIB, other // SIB] = z[at]

                    @pl.when(on_col & (other % SIB == f.r))
                    def _():
                        out[other // SIB, node // SIB] = z[at].T

            if corner:

                @pl.when(on_row & on_col)
                def _():
                    out[node // SIB, node // SIB] = z[count]


def square_plan(top_inverse, upper_factor, pivot_inverse, widths, order, pattern):
    row_rank = lax.axis_index("row")
    col_rank = lax.axis_index("col")
    size = top_inverse.shape[-1]
    total, window = widths.shape[0], order.shape[0]
    levels = window // SIB
    near = window // SIB
    bf16 = jnp.bfloat16
    dims = (window, total)

    def blocks(*lead, dtype=bf16):
        return jax.ShapeDtypeStruct((*lead, size, size), dtype)

    unit = 2 * size**3
    ranks = jnp.stack([row_rank, col_rank]).astype(jnp.int32)
    sc = jnp.concatenate([ranks, order, pattern.reshape(-1), widths])
    known = top_inverse[:, 0, :, 0]
    factor = upper_factor[:, 0, :, 0]
    tops = row_pieces(factor[:, near:])
    groups = [(0, 1), (1, 1), (2, levels - 2)]
    parts = [
        call(
            functools.partial(top_product, first),
            dims,
            sc,
            [known, *tops],
            [blocks(levels, SIB * count)],
            scratch=[
                pltpu.VMEM((SIB * count, levels, size, size), bf16),
                pltpu.VMEM((SIB * count, size, levels * size), bf16),
                pltpu.SemaphoreType.DMA((SIB * count,)),
            ],
            hbm=(1, 2, 3, 4),
            flops=64 * count * unit,
        )[0]
        for first, count in groups
    ]
    fence = lax.optimization_barrier
    sums = []
    for part, (_, count) in zip(parts, groups):
        total_part = lax.psum_scatter(part, "col", scatter_dimension=0)
        sums += [(total_part, at * SIB) for at in range(count)]
    wins = row_pieces(factor[:, :near])
    tops, wins, _ = fence((tops, wins, parts))
    own = call(
        functools.partial(own_blocks, levels),
        dims,
        sc,
        [*tops, *wins],
        [blocks(levels)] * SIB + [blocks(near)] * (levels - 1),
        scratch=[pltpu.SemaphoreType.DMA((levels, SIB + 1))],
        hbm=tuple(range(8)),
    )
    own = list(own)

    def flat(lists):
        return [x for xs in lists for x in xs]

    def top_level(l):
        ys = []
        for d in range(SIB):
            share = lax.dynamic_index_in_dim(sums[l][0], sums[l][1] + (row_rank ^ d), 0, keepdims=False)
            ys.append(swap(share, "row", d) if d else share)
        return call(
            functools.partial(top_column, l),
            dims,
            sc,
            ys + flat(columns) + ([wide[l]] if l else []),
            [blocks(SIB)],
            flops=16 * l * unit,
        )[0]

    def later_products(l):
        (right,) = call(
            functools.partial(cross_product, l, levels),
            dims,
            sc,
            [*columns[l], *crossing],
            [blocks(SIB * (levels - 1 - l) + 1)],
            flops=16 * (levels - 1 - l) * unit,
        )
        return col_sum(right)

    def window_level(k, low, high):
        whole = low == 0 and high == k
        outs = [blocks(SIB * (high - low) + whole)]
        if not whole:
            outs.append(blocks(1, dtype=jnp.float32))
        return call(
            functools.partial(window_column, k, low, high),
            dims,
            sc,
            rights[low : high + whole] + flat(solved) + ([wide[k]] if k else []) + ([pivot] if whole else []),
            outs,
            scratch=[pltpu.VMEM((SIB * k, size, size), bf16)] if k else [],
            flops=SIB * (high - low) * (SIB * k - 2) * unit,
        )

    columns, wide, rights, solved = [], [None], [], []
    wide.append(col_pieces(own[SIB]))
    columns.append(row_pieces(top_level(0)))
    columns, wide, own = fence((columns, wide, own))
    crossing = [own[0]] + [swap(own[s], "col", s) for s in range(1, SIB)]
    wide.append(col_pieces(own[SIB + 1]))
    columns.append(row_pieces(top_level(1)))
    columns, wide, own, crossing = fence((columns, wide, own, crossing))
    rights.append(later_products(0))
    wide.append(col_pieces(own[SIB + 2]))
    columns.append(row_pieces(top_level(2)))
    columns, wide, crossing = fence((columns, wide, crossing))
    rights.append(later_products(1))
    pivs = row_pieces(pivot_inverse[:, 0].astype(bf16))
    (pivot,) = call(functools.partial(own_pivots, levels), dims, sc, pivs, [blocks(levels)])
    solved.append(row_pieces(window_level(0, 0, 0)[0]))
    columns.append(row_pieces(top_level(3)))
    columns, crossing, rights, solved, pivot = fence((columns, crossing, rights, solved, pivot))
    rights.append(later_products(2))
    (top_sum,) = call(
        functools.partial(cross_product, 3, levels), dims, sc, [*columns[3], *crossing], [blocks(1)], flops=4 * unit
    )
    top_sum = col_sum(top_sum)
    starts = [(0, 0, 0, True)]
    for k in range(1, levels - 1):
        solved.append(row_pieces(window_level(k, 0, k)[0]))
        starts.append((k, 0, SIB * k, True))
    k = levels - 1
    early, early_share = window_level(k, 0, k - 1)
    late, late_share = window_level(k, k - 1, k)
    (corner,) = call(
        functools.partial(pivot_block, k), dims, sc, [pivot, top_sum, early_share, late_share], [blocks(1)]
    )
    solved.append(row_pieces(early))
    starts.append((k, 0, SIB * (k - 1), False))
    solved.append(row_pieces(late))
    starts.append((k, k - 1, SIB, False))
    solved.append([swap(corner, "row", d) if d else corner for d in range(SIB)])
    starts.append((k, 0, 0, True))

    packed = call(
        functools.partial(pack_rows, levels),
        dims,
        sc,
        flat(columns),
        [blocks(levels)] * SIB,
        scratch=[pltpu.SemaphoreType.DMA((levels, SIB))],
        hbm=tuple(range(SIB * levels)),
    )
    rows = [packed[0]] + [swap(packed[s], "col", s) for s in range(1, SIB)]
    (out,) = call(
        functools.partial(place, starts),
        dims,
        sc,
        rows + flat(solved),
        [blocks(total // SIB, levels)],
    )
    return out[:, None, :, None]


def solution(mesh):
    in_specs = (
        P("pole", "row", None, "col", None, None),
        P("pole", "row", None, "col", None, None),
        P("pole", "row", None, None),
        P(),
        P(),
        P(),
    )
    out_specs = P("pole", "row", None, "col", None, None)
    square = mesh.shape["row"] == SIB and mesh.shape["col"] == SIB
    return jax.shard_map(
        square_plan if square else per_device, mesh=mesh, in_specs=in_specs, out_specs=out_specs, check_vma=False
    )
```

```python
import functools

import jax
import jax.numpy as jnp
from jax import lax
from jax.experimental import pallas as pl
from jax.experimental.pallas import tpu as pltpu
from jax.sharding import PartitionSpec as P

SIB = 4


def from_root(x, axis, root):
    mine = lax.axis_index(axis) == root
    return lax.psum(jnp.where(mine, x, jnp.zeros_like(x)), axis)


def per_device(top_inverse, upper_factor, pivot_inverse, widths, order, pattern):
    row_count = lax.axis_size("row")
    col_count = lax.axis_size("col")
    row_rank = lax.axis_index("row")
    col_rank = lax.axis_index("col")
    tile_size = top_inverse.shape[-1]
    total_nodes = widths.shape[0]
    window = order.shape[0]
    row_blocks = total_nodes // row_count
    col_blocks = total_nodes // col_count
    row_span = row_count // col_count
    factor = upper_factor[:, 0, :, 0]
    pivots = pivot_inverse[:, 0]
    live_rows = (
        lax.broadcasted_iota(jnp.int32, (total_nodes, tile_size), 1) < widths[:, None]
    ).astype(jnp.bfloat16)
    row_nodes = jnp.arange(row_blocks, dtype=jnp.int32) * row_count + row_rank
    col_nodes = jnp.arange(col_blocks, dtype=jnp.int32) * col_count + col_rank
    blocks_held = jnp.zeros((row_blocks, col_blocks, tile_size, tile_size), jnp.bfloat16)
    blocks_held = blocks_held.at[window // row_count :, window // col_count :].set(
        top_inverse[:, 0, :, 0]
    )
    members = SIB

    def fetch(node_id):
        local_rows = lax.dynamic_index_in_dim(factor, node_id // row_count, 0, keepdims=False)
        return from_root(local_rows, "row", node_id % row_count)

    def panel(node_id):
        received = fetch(node_id)
        present = pattern[col_nodes, node_id].astype(jnp.bfloat16)
        keep_mask = (
            present[:, None, None]
            * live_rows[col_nodes][:, None, :]
            * live_rows[node_id][None, :, None]
        )
        return received * keep_mask

    def step(position, blocks_held):
        node_ids = lax.dynamic_slice_in_dim(order, position * members, members)
        node_list = [node_ids[member] for member in range(members)]
        panels = jnp.stack([panel(node_id) for node_id in node_list])
        partial_value = jnp.einsum(
            "abpq,ibsq->iaps", blocks_held, panels, preferred_element_type=jnp.float32
        )
        summed = lax.psum_scatter(
            partial_value.astype(jnp.bfloat16), "col", scatter_dimension=2, tiled=True
        ).astype(jnp.float32)
        row_share = (-summed).astype(jnp.bfloat16)
        column_new = lax.all_gather(row_share, "col", axis=2, tiled=True)
        present = jnp.transpose(pattern[row_nodes][:, node_ids]).astype(jnp.bfloat16)
        node_live = live_rows[node_ids]
        column_mask = (
            present[:, :, None, None]
            * live_rows[row_nodes][None, :, :, None]
            * node_live[:, None, None, :]
        )
        column_new = column_new * column_mask
        for member, node_id in enumerate(node_list):
            column_at = node_id // col_count
            current = lax.dynamic_slice_in_dim(blocks_held, column_at, 1, 1)
            update = jnp.where(
                col_rank == node_id % col_count, column_new[member][:, None], current
            )
            blocks_held = lax.dynamic_update_slice_in_dim(blocks_held, update, column_at, 1)
        arrived = []
        for offset in range(row_span):
            arrived.append(from_root(column_new, "row", col_rank + offset * col_count))
        mirror = jnp.stack(arrived, 2).reshape(members, row_blocks * row_span, tile_size, tile_size)
        pivot_part = jnp.einsum(
            "ibsq,ibqt->ist", panels, mirror, preferred_element_type=jnp.float32
        )
        pivot_total = lax.psum(pivot_part.astype(jnp.bfloat16), "col").astype(jnp.float32)
        for member, node_id in enumerate(node_list):
            row_at = node_id // row_count
            column_at = node_id // col_count
            on_row = row_rank == node_id % row_count
            on_col = col_rank == node_id % col_count
            current = lax.dynamic_slice_in_dim(blocks_held, row_at, 1, 0)
            flipped = jnp.swapaxes(mirror[member], 1, 2)[None]
            update = jnp.where(on_row, flipped, current)
            own_pivot = lax.dynamic_index_in_dim(pivots, row_at, 0, keepdims=False)
            corner_mask = node_live[member][:, None].astype(jnp.float32) * node_live[member][
                None, :
            ].astype(jnp.float32)
            corner = ((own_pivot - pivot_total[member]) * corner_mask).astype(jnp.bfloat16)
            update = update.at[0, column_at].set(
                jnp.where(on_row & on_col, corner, update[0, column_at])
            )
            blocks_held = lax.dynamic_update_slice_in_dim(blocks_held, update, row_at, 0)
        return blocks_held

    blocks_held = lax.fori_loop(0, window // members, step, blocks_held)
    return blocks_held[:, : window // col_count][:, None, :, None]


VMEM_BYTES = 50 * 1024 * 1024
ORD = 2


def dot_nt(a, b):
    return lax.dot_general(a, b, (((1,), (1,)), ((), ())), preferred_element_type=jnp.float32)


def dot_nn(a, b):
    return jnp.dot(a, b, preferred_element_type=jnp.float32)


class Facts:
    def __init__(self, sc, window, total):
        self.sc, self.window = sc, window
        self.pat_at = ORD + window
        self.wid_at = self.pat_at + window * total
        self.r, self.c = sc[0], sc[1]

    def node(self, level, member):
        return self.sc[ORD + level * SIB + member]

    def pat(self, row, col):
        return self.sc[self.pat_at + row * self.window + col]

    def width(self, node):
        return self.sc[self.wid_at + node]


def keep(x, rows, cols):
    at_row = lax.broadcasted_iota(jnp.int32, x.shape, 0)
    at_col = lax.broadcasted_iota(jnp.int32, x.shape, 1)
    return jnp.where((at_row < rows) & (at_col < cols), x, 0.0)


def call(body, dims, sc, inputs, outs, scratch=(), hbm=(), flops=0):
    specs = [pl.BlockSpec(memory_space=pltpu.SMEM)]
    for at in range(len(inputs)):
        specs.append(pl.BlockSpec(memory_space=pl.ANY if at in hbm else pltpu.VMEM))
    moved = sum(x.size * x.dtype.itemsize for x in list(inputs) + list(outs))

    def kernel(sc_ref, *refs):
        body(Facts(sc_ref, *dims), *refs)

    return pl.pallas_call(
        kernel,
        out_shape=list(outs),
        in_specs=specs,
        out_specs=[pl.BlockSpec(memory_space=pltpu.VMEM)] * len(outs),
        scratch_shapes=list(scratch),
        compiler_params=pltpu.CompilerParams(vmem_limit_bytes=VMEM_BYTES),
        cost_estimate=pl.CostEstimate(flops=flops, bytes_accessed=moved, transcendentals=0),
    )(sc, *inputs)


def swap(x, axis, d):
    count = lax.axis_size(axis)
    return lax.ppermute(x, axis, [(i, i ^ d) for i in range(count)])


def row_pieces(x):
    far = swap(x, "row", 2)
    return [x, swap(x, "row", 1), far, swap(far, "row", 1)]


def col_pieces(x):
    rank = lax.axis_index("col")
    last = SIB - 1
    up, down = [x], [x]
    for hop in range(1, SIB):
        down.append(lax.ppermute(down[-1], "col", [(i + 1, i) for i in range(SIB - hop)]))
        up.append(lax.ppermute(up[-1], "col", [(i, i + 1) for i in range(hop - 1, last)]))
    one = jnp.where(rank % 2 == 0, down[1], up[1])
    two = jnp.where(rank < 2, down[2], up[2])
    lower = jnp.where(rank == 0, down[3], down[1])
    upper = jnp.where(rank == last, up[3], up[1])
    return jnp.stack([x, one, two, jnp.where(rank < 2, lower, upper)])


def col_sum(x):
    last = SIB - 1
    at_end = (lax.axis_index("col") == 0) | (lax.axis_index("col") == last)

    def add(a, b):
        return (a.astype(jnp.float32) + b.astype(jnp.float32)).astype(jnp.bfloat16)

    half = add(x, lax.ppermute(x, "col", [(0, 1), (last, last - 1)]))
    full = add(half, lax.ppermute(half, "col", [(1, 2), (2, 1)]))
    return jnp.where(at_end, lax.ppermute(full, "col", [(1, 0), (last - 1, last)]), full)


def top_product(first, f, h, u0, u1, u2, u3, out, ubuf, lbuf, sems):
    pieces = (u0, u1, u2, u3)
    size = h.shape[-1]
    depth = h.shape[1]
    count = out.shape[1]
    for m in range(count):
        node = f.node(first, m)
        for d in range(SIB):

            @pl.when((node % SIB) ^ f.r == d)
            def _():
                pltpu.make_async_copy(pieces[d].at[node // SIB], ubuf.at[m], sems.at[m]).start()

    for m in range(count):
        node = f.node(first, m)
        pltpu.make_async_copy(u0.at[0], ubuf.at[m], sems.at[m]).wait()
        for b in range(depth):
            at = f.window + b * SIB + f.c
            reach = jnp.where(f.pat(at, node) > 0, f.width(at), 0)
            kept = keep(ubuf[m, b].astype(jnp.float32), size, reach)
            lbuf[m, :, b * size : (b + 1) * size] = kept.astype(jnp.bfloat16)
    for a in range(h.shape[0]):
        rows = jnp.concatenate([h[a, b] for b in range(depth)], axis=1)
        for m in range(count):
            out[a, m] = dot_nt(rows, lbuf[m]).astype(jnp.bfloat16)


def own_blocks(levels, f, *refs):
    tops, wins = refs[0:4], refs[4:8]
    by_slice, by_level = refs[8:12], refs[12 : 11 + levels]
    sems = refs[11 + levels]
    for wait in (False, True):
        for k in range(levels):
            node = f.node(k, f.r)
            at = node // SIB
            source = (node % SIB) ^ f.r
            for d in range(SIB):
                copies = [
                    pltpu.make_async_copy(tops[d].at[at, f.c ^ s], by_slice[s].at[k], sems.at[k, s])
                    for s in range(SIB)
                ]
                if k:
                    copies.append(
                        pltpu.make_async_copy(wins[d].at[at], by_level[k - 1], sems.at[k, SIB])
                    )

                @pl.when(source == d)
                def _():
                    for copy in copies:
                        if wait:
                            copy.wait()
                        else:
                            copy.start()


def own_pivots(levels, f, p0, p1, p2, p3, out):
    pieces = (p0, p1, p2, p3)
    for k in range(levels):
        node = f.node(k, f.r)
        for d in range(SIB):

            @pl.when((node % SIB) ^ f.r == d)
            def _():
                out[k] = pieces[d][node // SIB]


def wide_at(level):
    return max(level - 2, 0) * SIB


def top_column(level, f, *refs):
    ys = refs[0:SIB]
    earlier = refs[SIB : SIB + SIB * level]
    out = refs[-1]
    node = f.node(level, f.r)
    acc = [y[...].astype(jnp.float32) for y in ys]
    if level:
        lw = refs[-2]
        for j in range(level):
            for d in range(SIB):
                at = f.node(j, f.r ^ d)
                block = lw[(at % SIB) ^ f.c, wide_at(level) + at // SIB]
                block = jnp.where(f.pat(at, node) > 0, block, jnp.zeros_like(block))
                for e in range(SIB):
                    acc[e] += dot_nt(earlier[j * SIB + d][d ^ e], block)
    for e in range(SIB):
        row = f.window + f.c * SIB + (f.r ^ e)
        reach = jnp.where(f.pat(row, node) > 0, f.width(row), 0)
        out[e] = keep(-acc[e], reach, f.width(node)).astype(jnp.bfloat16)


def cross_product(level, levels, f, *refs):
    xs, ts, out = refs[0:4], refs[4:8], refs[8]
    turn = f.c ^ f.r
    for k in range(level, levels):
        node = f.node(k, f.r)
        parts = []
        for s in range(SIB):
            row = f.window + f.c * SIB + (f.c ^ s)
            block = ts[s][k]
            parts.append(jnp.where(f.pat(row, node) > 0, block, jnp.zeros_like(block)))
        left = jnp.concatenate(parts, axis=1)
        for d in range(SIB if k > level else 1):
            right = jnp.concatenate([xs[d][turn ^ (s ^ d)] for s in range(SIB)], axis=0)
            at = (k - level - 1) * SIB + d if k > level else (levels - 1 - level) * SIB
            out[at] = dot_nn(left, right).astype(jnp.bfloat16)


def window_column(k, low, high, f, *refs):
    whole = low == 0 and high == k
    count = high - low + whole
    vs = refs[0:count]
    zs = [refs[count + SIB * i : count + SIB * (i + 1)] for i in range(k)]
    at = count + SIB * k
    node = f.node(k, f.r)
    width = f.width(node)
    if k:
        lw, ub = refs[at], refs[-1]
        at += 1
    if whole:
        piv, out = refs[at], refs[at + 1]
        total = vs[-1][vs[-1].shape[0] - 1].astype(jnp.float32)
    else:
        out, share = refs[at], refs[at + 1]
        total = jnp.zeros(ub.shape[1:], jnp.float32)
    for i in range(k):
        for d in range(SIB):
            at = f.node(i, f.r ^ d)
            block = lw[(at % SIB) ^ f.c, wide_at(k) + at // SIB]
            ub[i * SIB + d] = jnp.where(f.pat(at, node) > 0, block, jnp.zeros_like(block))
    for j in range(low, high):
        for d in range(SIB):
            acc = vs[j - low][(k - j - 1) * SIB + d].astype(jnp.float32)
            for i in range(k):
                for e in range(SIB):
                    left = ub[i * SIB + e]
                    if i > j:
                        acc += dot_nn(left, zs[i][e][j * SIB + (d ^ e)])
                    elif i < j:
                        acc += dot_nt(left, zs[j][d][i * SIB + (d ^ e)])
                    elif d == e:
                        acc += dot_nt(left, zs[j][d][j * SIB])
            at = f.node(j, f.r ^ d)
            reach = jnp.where(f.pat(at, node) > 0, f.width(at), 0)
            block = keep(-acc, width, reach).astype(jnp.bfloat16)
            out[(j - low) * SIB + d] = block
            total += dot_nt(ub[j * SIB + d], block)
    if whole:
        corner = piv[k].astype(jnp.float32) - total
        out[k * SIB] = keep(corner, width, width).astype(jnp.bfloat16)
    else:
        share[0] = total


def pivot_block(k, f, piv, top_sum, *refs):
    out = refs[-1]
    total = top_sum[0].astype(jnp.float32)
    for part in refs[:-1]:
        total += part[0]
    width = f.width(f.node(k, f.r))
    out[0] = keep(piv[k].astype(jnp.float32) - total, width, width).astype(jnp.bfloat16)


def pack_rows(levels, f, *refs):
    xs, outs, sems = refs[: SIB * levels], refs[SIB * levels : SIB * levels + SIB], refs[-1]
    for wait in (False, True):
        for l in range(levels):
            for d in range(SIB):
                node = f.node(l, f.r ^ d)
                for s in range(SIB):

                    @pl.when((node % SIB) ^ f.c == s)
                    def _():
                        copy = pltpu.make_async_copy(
                            xs[l * SIB + d].at[d], outs[s].at[node // SIB], sems.at[l, d]
                        )
                        if wait:
                            copy.wait()
                        else:
                            copy.start()


def place(starts, f, *refs):
    rows, out = refs[0:SIB], refs[-1]
    top = out.shape[0] // 2
    for s in range(SIB):
        out[top + (f.c ^ s)] = rows[s][...]
    out[0:top] = jnp.zeros_like(out[0:top])
    for at, (k, low, count, corner) in enumerate(starts):
        for d in range(SIB):
            z = refs[SIB + at * SIB + d]
            node = f.node(k, f.r ^ d)
            on_row, on_col = node % SIB == f.r, node % SIB == f.c
            if count:

                @pl.loop(0, count)
                def _(at):
                    other = f.node(low + at // SIB, f.r ^ d ^ (at % SIB))

                    @pl.when(on_row & (other % SIB == f.c))
                    def _():
                        out[node // SIB, other // SIB] = z[at]

                    @pl.when(on_col & (other % SIB == f.r))
                    def _():
                        out[other // SIB, node // SIB] = z[at].T

            if corner:

                @pl.when(on_row & on_col)
                def _():
                    out[node // SIB, node // SIB] = z[count]


def square_plan(top_inverse, upper_factor, pivot_inverse, widths, order, pattern):
    row_rank = lax.axis_index("row")
    col_rank = lax.axis_index("col")
    size = top_inverse.shape[-1]
    total, window = widths.shape[0], order.shape[0]
    levels = window // SIB
    near = window // SIB
    bf16 = jnp.bfloat16
    dims = (window, total)

    def blocks(*lead, dtype=bf16):
        return jax.ShapeDtypeStruct((*lead, size, size), dtype)

    unit = 2 * size**3
    ranks = jnp.stack([row_rank, col_rank]).astype(jnp.int32)
    sc = jnp.concatenate([ranks, order, pattern.reshape(-1), widths])
    known = top_inverse[:, 0, :, 0]
    factor = upper_factor[:, 0, :, 0]
    tops = row_pieces(factor[:, near:])
    groups = [(0, 1), (1, 1), (2, levels - 2)]
    parts = [
        call(
            functools.partial(top_product, first),
            dims,
            sc,
            [known, *tops],
            [blocks(levels, SIB * count)],
            scratch=[
                pltpu.VMEM((SIB * count, levels, size, size), bf16),
                pltpu.VMEM((SIB * count, size, levels * size), bf16),
                pltpu.SemaphoreType.DMA((SIB * count,)),
            ],
            hbm=(1, 2, 3, 4),
            flops=64 * count * unit,
        )[0]
        for first, count in groups
    ]
    fence = lax.optimization_barrier
    sums = []
    for part, (_, count) in zip(parts, groups):
        total_part = lax.psum_scatter(part, "col", scatter_dimension=0)
        sums += [(total_part, at * SIB) for at in range(count)]
    wins = row_pieces(factor[:, :near])
    tops, wins, _ = fence((tops, wins, parts))
    own = call(
        functools.partial(own_blocks, levels),
        dims,
        sc,
        [*tops, *wins],
        [blocks(levels)] * SIB + [blocks(near)] * (levels - 1),
        scratch=[pltpu.SemaphoreType.DMA((levels, SIB + 1))],
        hbm=tuple(range(8)),
    )
    own = list(own)

    def flat(lists):
        return [x for xs in lists for x in xs]

    def top_level(l):
        ys = []
        for d in range(SIB):
            share = lax.dynamic_index_in_dim(sums[l][0], sums[l][1] + (row_rank ^ d), 0, keepdims=False)
            ys.append(swap(share, "row", d) if d else share)
        return call(
            functools.partial(top_column, l),
            dims,
            sc,
            ys + flat(columns) + ([wide[l]] if l else []),
            [blocks(SIB)],
            flops=16 * l * unit,
        )[0]

    def later_products(l):
        (right,) = call(
            functools.partial(cross_product, l, levels),
            dims,
            sc,
            [*columns[l], *crossing],
            [blocks(SIB * (levels - 1 - l) + 1)],
            flops=16 * (levels - 1 - l) * unit,
        )
        share = lax.psum_scatter(right, "col", scatter_dimension=1, tiled=True)
        return lax.all_gather(share, "col", axis=1, tiled=True)

    def window_level(k, low, high):
        whole = low == 0 and high == k
        outs = [blocks(SIB * (high - low) + whole)]
        if not whole:
            outs.append(blocks(1, dtype=jnp.float32))
        return call(
            functools.partial(window_column, k, low, high),
            dims,
            sc,
            rights[low : high + whole] + flat(solved) + ([wide[k]] if k else []) + ([pivot] if whole else []),
            outs,
            scratch=[pltpu.VMEM((SIB * k, size, size), bf16)] if k else [],
            flops=SIB * (high - low) * (SIB * k - 2) * unit,
        )

    columns, wide, rights, solved = [], [None], [], []
    crossing = [own[0]] + [swap(own[s], "col", s) for s in range(1, SIB)]
    wide.append(col_pieces(own[SIB]))
    columns.append(row_pieces(top_level(0)))
    columns, wide, own, crossing = fence((columns, wide, own, crossing))
    rights.append(later_products(0))
    last_wide = col_pieces(jnp.concatenate(own[SIB + 1 : SIB + levels - 1]))
    wide += [last_wide] * (levels - 2)
    columns.append(row_pieces(top_level(1)))
    rights.append(later_products(1))
    pivs = row_pieces(pivot_inverse[:, 0].astype(bf16))
    (pivot,) = call(functools.partial(own_pivots, levels), dims, sc, pivs, [blocks(levels)])
    columns, wide, crossing, pivot = fence((columns, wide, crossing, pivot))
    columns.append(row_pieces(top_level(2)))
    rights.append(later_products(2))
    columns.append(row_pieces(top_level(3)))
    solved.append(row_pieces(window_level(0, 0, 0)[0]))
    columns, crossing, late_pivot = fence((columns, crossing, pivot))
    (top_sum,) = call(
        functools.partial(cross_product, 3, levels), dims, sc, [*columns[3], *crossing], [blocks(1)], flops=4 * unit
    )
    top_sum = col_sum(top_sum)
    starts = [(0, 0, 0, True)]
    for k in range(1, levels - 1):
        pivot = pivot if k < levels - 2 else late_pivot
        solved.append(row_pieces(window_level(k, 0, k)[0]))
        starts.append((k, 0, SIB * k, True))
    k = levels - 1
    early, early_share = window_level(k, 0, k - 1)
    late, late_share = window_level(k, k - 1, k)
    (corner,) = call(
        functools.partial(pivot_block, k), dims, sc, [pivot, top_sum, early_share, late_share], [blocks(1)]
    )
    solved.append(row_pieces(early))
    starts.append((k, 0, SIB * (k - 1), False))
    solved.append(row_pieces(late))
    starts.append((k, k - 1, SIB, False))
    solved.append([swap(corner, "row", d) if d else corner for d in range(SIB)])
    starts.append((k, 0, 0, True))

    packed = call(
        functools.partial(pack_rows, levels),
        dims,
        sc,
        flat(columns),
        [blocks(levels)] * SIB,
        scratch=[pltpu.SemaphoreType.DMA((levels, SIB))],
        hbm=tuple(range(SIB * levels)),
    )
    rows = [packed[0]] + [swap(packed[s], "col", s) for s in range(1, SIB)]
    (out,) = call(
        functools.partial(place, starts),
        dims,
        sc,
        rows + flat(solved),
        [blocks(total // SIB, levels)],
    )
    return out[:, None, :, None]


def solution(mesh):
    in_specs = (
        P("pole", "row", None, "col", None, None),
        P("pole", "row", None, "col", None, None),
        P("pole", "row", None, None),
        P(),
        P(),
        P(),
    )
    out_specs = P("pole", "row", None, "col", None, None)
    square = mesh.shape["row"] == SIB and mesh.shape["col"] == SIB
    return jax.shard_map(
        square_plan if square else per_device, mesh=mesh, in_specs=in_specs, out_specs=out_specs, check_vma=False
    )
```

```python
import functools

import jax
import jax.numpy as jnp
from jax import lax
from jax.experimental import pallas as pl
from jax.experimental.pallas import tpu as pltpu
from jax.sharding import PartitionSpec as P

SIB = 4


def from_root(x, axis, root):
    mine = lax.axis_index(axis) == root
    return lax.psum(jnp.where(mine, x, jnp.zeros_like(x)), axis)


def per_device(top_inverse, upper_factor, pivot_inverse, widths, order, pattern):
    row_count = lax.axis_size("row")
    col_count = lax.axis_size("col")
    row_rank = lax.axis_index("row")
    col_rank = lax.axis_index("col")
    tile_size = top_inverse.shape[-1]
    total_nodes = widths.shape[0]
    window = order.shape[0]
    row_blocks = total_nodes // row_count
    col_blocks = total_nodes // col_count
    row_span = row_count // col_count
    factor = upper_factor[:, 0, :, 0]
    pivots = pivot_inverse[:, 0]
    live_rows = (
        lax.broadcasted_iota(jnp.int32, (total_nodes, tile_size), 1) < widths[:, None]
    ).astype(jnp.bfloat16)
    row_nodes = jnp.arange(row_blocks, dtype=jnp.int32) * row_count + row_rank
    col_nodes = jnp.arange(col_blocks, dtype=jnp.int32) * col_count + col_rank
    blocks_held = jnp.zeros((row_blocks, col_blocks, tile_size, tile_size), jnp.bfloat16)
    blocks_held = blocks_held.at[window // row_count :, window // col_count :].set(
        top_inverse[:, 0, :, 0]
    )
    members = SIB

    def fetch(node_id):
        local_rows = lax.dynamic_index_in_dim(factor, node_id // row_count, 0, keepdims=False)
        return from_root(local_rows, "row", node_id % row_count)

    def panel(node_id):
        received = fetch(node_id)
        present = pattern[col_nodes, node_id].astype(jnp.bfloat16)
        keep_mask = (
            present[:, None, None]
            * live_rows[col_nodes][:, None, :]
            * live_rows[node_id][None, :, None]
        )
        return received * keep_mask

    def step(position, blocks_held):
        node_ids = lax.dynamic_slice_in_dim(order, position * members, members)
        node_list = [node_ids[member] for member in range(members)]
        panels = jnp.stack([panel(node_id) for node_id in node_list])
        partial_value = jnp.einsum(
            "abpq,ibsq->iaps", blocks_held, panels, preferred_element_type=jnp.float32
        )
        summed = lax.psum_scatter(
            partial_value.astype(jnp.bfloat16), "col", scatter_dimension=2, tiled=True
        ).astype(jnp.float32)
        row_share = (-summed).astype(jnp.bfloat16)
        column_new = lax.all_gather(row_share, "col", axis=2, tiled=True)
        present = jnp.transpose(pattern[row_nodes][:, node_ids]).astype(jnp.bfloat16)
        node_live = live_rows[node_ids]
        column_mask = (
            present[:, :, None, None]
            * live_rows[row_nodes][None, :, :, None]
            * node_live[:, None, None, :]
        )
        column_new = column_new * column_mask
        for member, node_id in enumerate(node_list):
            column_at = node_id // col_count
            current = lax.dynamic_slice_in_dim(blocks_held, column_at, 1, 1)
            update = jnp.where(
                col_rank == node_id % col_count, column_new[member][:, None], current
            )
            blocks_held = lax.dynamic_update_slice_in_dim(blocks_held, update, column_at, 1)
        arrived = []
        for offset in range(row_span):
            arrived.append(from_root(column_new, "row", col_rank + offset * col_count))
        mirror = jnp.stack(arrived, 2).reshape(members, row_blocks * row_span, tile_size, tile_size)
        pivot_part = jnp.einsum(
            "ibsq,ibqt->ist", panels, mirror, preferred_element_type=jnp.float32
        )
        pivot_total = lax.psum(pivot_part.astype(jnp.bfloat16), "col").astype(jnp.float32)
        for member, node_id in enumerate(node_list):
            row_at = node_id // row_count
            column_at = node_id // col_count
            on_row = row_rank == node_id % row_count
            on_col = col_rank == node_id % col_count
            current = lax.dynamic_slice_in_dim(blocks_held, row_at, 1, 0)
            flipped = jnp.swapaxes(mirror[member], 1, 2)[None]
            update = jnp.where(on_row, flipped, current)
            own_pivot = lax.dynamic_index_in_dim(pivots, row_at, 0, keepdims=False)
            corner_mask = node_live[member][:, None].astype(jnp.float32) * node_live[member][
                None, :
            ].astype(jnp.float32)
            corner = ((own_pivot - pivot_total[member]) * corner_mask).astype(jnp.bfloat16)
            update = update.at[0, column_at].set(
                jnp.where(on_row & on_col, corner, update[0, column_at])
            )
            blocks_held = lax.dynamic_update_slice_in_dim(blocks_held, update, row_at, 0)
        return blocks_held

    blocks_held = lax.fori_loop(0, window // members, step, blocks_held)
    return blocks_held[:, : window // col_count][:, None, :, None]


VMEM_BYTES = 50 * 1024 * 1024
ORD = 2


def dot_nt(a, b):
    return lax.dot_general(a, b, (((1,), (1,)), ((), ())), preferred_element_type=jnp.float32)


def dot_nn(a, b):
    return jnp.dot(a, b, preferred_element_type=jnp.float32)


class Facts:
    def __init__(self, sc, window, total):
        self.sc, self.window = sc, window
        self.pat_at = ORD + window
        self.wid_at = self.pat_at + window * total
        self.r, self.c = sc[0], sc[1]

    def node(self, level, member):
        return self.sc[ORD + level * SIB + member]

    def pat(self, row, col):
        return self.sc[self.pat_at + row * self.window + col]

    def width(self, node):
        return self.sc[self.wid_at + node]


def keep(x, rows, cols):
    at_row = lax.broadcasted_iota(jnp.int32, x.shape, 0)
    at_col = lax.broadcasted_iota(jnp.int32, x.shape, 1)
    return jnp.where((at_row < rows) & (at_col < cols), x, 0.0)


def call(body, dims, sc, inputs, outs, scratch=(), hbm=(), flops=0):
    specs = [pl.BlockSpec(memory_space=pltpu.SMEM)]
    for at in range(len(inputs)):
        specs.append(pl.BlockSpec(memory_space=pl.ANY if at in hbm else pltpu.VMEM))
    moved = sum(x.size * x.dtype.itemsize for x in list(inputs) + list(outs))

    def kernel(sc_ref, *refs):
        body(Facts(sc_ref, *dims), *refs)

    return pl.pallas_call(
        kernel,
        out_shape=list(outs),
        in_specs=specs,
        out_specs=[pl.BlockSpec(memory_space=pltpu.VMEM)] * len(outs),
        scratch_shapes=list(scratch),
        compiler_params=pltpu.CompilerParams(vmem_limit_bytes=VMEM_BYTES),
        cost_estimate=pl.CostEstimate(flops=flops, bytes_accessed=moved, transcendentals=0),
    )(sc, *inputs)


def swap(x, axis, d):
    count = lax.axis_size(axis)
    return lax.ppermute(x, axis, [(i, i ^ d) for i in range(count)])


def row_pieces(x):
    far = swap(x, "row", 2)
    return [x, swap(x, "row", 1), far, swap(far, "row", 1)]


def col_pieces(x):
    rank = lax.axis_index("col")
    last = SIB - 1
    up, down = [x], [x]
    for hop in range(1, SIB):
        down.append(lax.ppermute(down[-1], "col", [(i + 1, i) for i in range(SIB - hop)]))
        up.append(lax.ppermute(up[-1], "col", [(i, i + 1) for i in range(hop - 1, last)]))
    one = jnp.where(rank % 2 == 0, down[1], up[1])
    two = jnp.where(rank < 2, down[2], up[2])
    lower = jnp.where(rank == 0, down[3], down[1])
    upper = jnp.where(rank == last, up[3], up[1])
    return jnp.stack([x, one, two, jnp.where(rank < 2, lower, upper)])


def col_sum(x):
    last = SIB - 1
    at_end = (lax.axis_index("col") == 0) | (lax.axis_index("col") == last)

    def add(a, b):
        return (a.astype(jnp.float32) + b.astype(jnp.float32)).astype(jnp.bfloat16)

    half = add(x, lax.ppermute(x, "col", [(0, 1), (last, last - 1)]))
    full = add(half, lax.ppermute(half, "col", [(1, 2), (2, 1)]))
    return jnp.where(at_end, lax.ppermute(full, "col", [(1, 0), (last - 1, last)]), full)


def top_product(first, f, h, u0, u1, u2, u3, out, ubuf, lbuf, sems):
    pieces = (u0, u1, u2, u3)
    size = h.shape[-1]
    depth = h.shape[1]
    count = out.shape[1]
    for m in range(count):
        node = f.node(first, m)
        for d in range(SIB):

            @pl.when((node % SIB) ^ f.r == d)
            def _():
                pltpu.make_async_copy(pieces[d].at[node // SIB], ubuf.at[m], sems.at[m]).start()

    for m in range(count):
        node = f.node(first, m)
        pltpu.make_async_copy(u0.at[0], ubuf.at[m], sems.at[m]).wait()
        for b in range(depth):
            at = f.window + b * SIB + f.c
            reach = jnp.where(f.pat(at, node) > 0, f.width(at), 0)
            kept = keep(ubuf[m, b].astype(jnp.float32), size, reach)
            lbuf[m, :, b * size : (b + 1) * size] = kept.astype(jnp.bfloat16)
    for a in range(h.shape[0]):
        rows = jnp.concatenate([h[a, b] for b in range(depth)], axis=1)
        for m in range(count):
            out[a, m] = dot_nt(rows, lbuf[m]).astype(jnp.bfloat16)


def own_blocks(levels, f, *refs):
    tops, wins = refs[0:4], refs[4:8]
    by_slice, by_level, sems = refs[8:12], refs[12], refs[13]
    near = wins[0].shape[1]
    for wait in (False, True):
        for k in range(levels):
            node = f.node(k, f.r)
            at = node // SIB
            source = (node % SIB) ^ f.r
            for d in range(SIB):
                copies = [
                    pltpu.make_async_copy(tops[d].at[at, f.c ^ s], by_slice[s].at[k], sems.at[k, s])
                    for s in range(SIB)
                ]
                if k:
                    room = by_level.at[pl.ds((k - 1) * near, near)]
                    copies.append(pltpu.make_async_copy(wins[d].at[at], room, sems.at[k, SIB]))

                @pl.when(source == d)
                def _():
                    for copy in copies:
                        if wait:
                            copy.wait()
                        else:
                            copy.start()


def own_pivots(levels, f, p0, p1, p2, p3, out):
    pieces = (p0, p1, p2, p3)
    for k in range(levels):
        node = f.node(k, f.r)
        for d in range(SIB):

            @pl.when((node % SIB) ^ f.r == d)
            def _():
                out[k] = pieces[d][node // SIB]


def wide_at(level):
    return (level - 1) * SIB


def top_column(level, f, *refs):
    ys = refs[0:SIB]
    earlier = refs[SIB : SIB + SIB * level]
    out = refs[-1]
    node = f.node(level, f.r)
    acc = [y[...].astype(jnp.float32) for y in ys]
    if level:
        lw = refs[-2]
        for j in range(level):
            for d in range(SIB):
                at = f.node(j, f.r ^ d)
                block = lw[(at % SIB) ^ f.c, wide_at(level) + at // SIB]
                block = jnp.where(f.pat(at, node) > 0, block, jnp.zeros_like(block))
                for e in range(SIB):
                    acc[e] += dot_nt(earlier[j * SIB + d][d ^ e], block)
    for e in range(SIB):
        row = f.window + f.c * SIB + (f.r ^ e)
        reach = jnp.where(f.pat(row, node) > 0, f.width(row), 0)
        out[e] = keep(-acc[e], reach, f.width(node)).astype(jnp.bfloat16)


def cross_product(level, levels, f, *refs):
    xs, ts, out = refs[0:4], refs[4:8], refs[8]
    turn = f.c ^ f.r
    for k in range(level, levels):
        node = f.node(k, f.r)
        parts = []
        for s in range(SIB):
            row = f.window + f.c * SIB + (f.c ^ s)
            block = ts[s][k]
            parts.append(jnp.where(f.pat(row, node) > 0, block, jnp.zeros_like(block)))
        left = jnp.concatenate(parts, axis=1)
        for d in range(SIB if k > level else 1):
            right = jnp.concatenate([xs[d][turn ^ (s ^ d)] for s in range(SIB)], axis=0)
            at = (k - level - 1) * SIB + d if k > level else (levels - 1 - level) * SIB
            out[at] = dot_nn(left, right).astype(jnp.bfloat16)


def window_column(k, low, high, f, *refs):
    whole = low == 0 and high == k
    count = high - low + whole
    vs = refs[0:count]
    zs = [refs[count + SIB * i : count + SIB * (i + 1)] for i in range(k)]
    at = count + SIB * k
    node = f.node(k, f.r)
    width = f.width(node)
    if k:
        lw, ub = refs[at], refs[-1]
        at += 1
    if whole:
        piv, out = refs[at], refs[at + 1]
        total = vs[-1][vs[-1].shape[0] - 1].astype(jnp.float32)
    else:
        out, share = refs[at], refs[at + 1]
        total = jnp.zeros(ub.shape[1:], jnp.float32)
    for i in range(k):
        for d in range(SIB):
            at = f.node(i, f.r ^ d)
            block = lw[(at % SIB) ^ f.c, wide_at(k) + at // SIB]
            ub[i * SIB + d] = jnp.where(f.pat(at, node) > 0, block, jnp.zeros_like(block))
    for j in range(low, high):
        for d in range(SIB):
            acc = vs[j - low][(k - j - 1) * SIB + d].astype(jnp.float32)
            for i in range(k):
                for e in range(SIB):
                    left = ub[i * SIB + e]
                    if i > j:
                        acc += dot_nn(left, zs[i][e][j * SIB + (d ^ e)])
                    elif i < j:
                        acc += dot_nt(left, zs[j][d][i * SIB + (d ^ e)])
                    elif d == e:
                        acc += dot_nt(left, zs[j][d][j * SIB])
            at = f.node(j, f.r ^ d)
            reach = jnp.where(f.pat(at, node) > 0, f.width(at), 0)
            block = keep(-acc, width, reach).astype(jnp.bfloat16)
            out[(j - low) * SIB + d] = block
            total += dot_nt(ub[j * SIB + d], block)
    if whole:
        corner = piv[k].astype(jnp.float32) - total
        out[k * SIB] = keep(corner, width, width).astype(jnp.bfloat16)
    else:
        share[0] = total


def pivot_block(k, f, piv, top_sum, *refs):
    out = refs[-1]
    total = top_sum[0].astype(jnp.float32)
    for part in refs[:-1]:
        total += part[0]
    width = f.width(f.node(k, f.r))
    out[0] = keep(piv[k].astype(jnp.float32) - total, width, width).astype(jnp.bfloat16)


def pack_rows(levels, f, *refs):
    xs, outs, sems = refs[: SIB * levels], refs[SIB * levels : SIB * levels + SIB], refs[-1]
    for wait in (False, True):
        for l in range(levels):
            for d in range(SIB):
                node = f.node(l, f.r ^ d)
                for s in range(SIB):

                    @pl.when((node % SIB) ^ f.c == s)
                    def _():
                        copy = pltpu.make_async_copy(
                            xs[l * SIB + d].at[d], outs[s].at[node // SIB], sems.at[l, d]
                        )
                        if wait:
                            copy.wait()
                        else:
                            copy.start()


def place(starts, f, *refs):
    rows, out = refs[0:SIB], refs[-1]
    top = out.shape[0] // 2
    for s in range(SIB):
        out[top + (f.c ^ s)] = rows[s][...]
    out[0:top] = jnp.zeros_like(out[0:top])
    for at, (k, low, count, corner) in enumerate(starts):
        for d in range(SIB):
            z = refs[SIB + at * SIB + d]
            node = f.node(k, f.r ^ d)
            on_row, on_col = node % SIB == f.r, node % SIB == f.c
            if count:

                @pl.loop(0, count)
                def _(at):
                    other = f.node(low + at // SIB, f.r ^ d ^ (at % SIB))

                    @pl.when(on_row & (other % SIB == f.c))
                    def _():
                        out[node // SIB, other // SIB] = z[at]

                    @pl.when(on_col & (other % SIB == f.r))
                    def _():
                        out[other // SIB, node // SIB] = z[at].T

            if corner:

                @pl.when(on_row & on_col)
                def _():
                    out[node // SIB, node // SIB] = z[count]


def square_plan(top_inverse, upper_factor, pivot_inverse, widths, order, pattern):
    row_rank = lax.axis_index("row")
    col_rank = lax.axis_index("col")
    size = top_inverse.shape[-1]
    total, window = widths.shape[0], order.shape[0]
    levels = window // SIB
    near = window // SIB
    bf16 = jnp.bfloat16
    dims = (window, total)

    def blocks(*lead, dtype=bf16):
        return jax.ShapeDtypeStruct((*lead, size, size), dtype)

    unit = 2 * size**3
    ranks = jnp.stack([row_rank, col_rank]).astype(jnp.int32)
    sc = jnp.concatenate([ranks, order, pattern.reshape(-1), widths])
    known = top_inverse[:, 0, :, 0]
    factor = upper_factor[:, 0, :, 0]
    tops = row_pieces(factor[:, near:])
    groups = [(0, 1), (1, levels - 1)]
    parts = [
        call(
            functools.partial(top_product, first),
            dims,
            sc,
            [known, *tops],
            [blocks(levels, SIB * count)],
            scratch=[
                pltpu.VMEM((SIB * count, levels, size, size), bf16),
                pltpu.VMEM((SIB * count, size, levels * size), bf16),
                pltpu.SemaphoreType.DMA((SIB * count,)),
            ],
            hbm=(1, 2, 3, 4),
            flops=64 * count * unit,
        )[0]
        for first, count in groups
    ]
    fence = lax.optimization_barrier
    sums = []
    for part, (_, count) in zip(parts, groups):
        total_part = lax.psum_scatter(part, "col", scatter_dimension=0)
        sums += [(total_part, at * SIB) for at in range(count)]
    window_factor, _ = fence((factor[:, :near], parts))
    wins = row_pieces(window_factor)
    own = call(
        functools.partial(own_blocks, levels),
        dims,
        sc,
        [*tops, *wins],
        [blocks(levels)] * SIB + [blocks((levels - 1) * near)],
        scratch=[pltpu.SemaphoreType.DMA((levels, SIB + 1))],
        hbm=tuple(range(8)),
    )
    own = list(own)

    def flat(lists):
        return [x for xs in lists for x in xs]

    def top_level(l):
        ys = []
        for d in range(SIB):
            share = lax.dynamic_index_in_dim(sums[l][0], sums[l][1] + (row_rank ^ d), 0, keepdims=False)
            ys.append(swap(share, "row", d) if d else share)
        return call(
            functools.partial(top_column, l),
            dims,
            sc,
            ys + flat(columns) + ([wide] if l else []),
            [blocks(SIB)],
            flops=16 * l * unit,
        )[0]

    def later_products(l):
        (right,) = call(
            functools.partial(cross_product, l, levels),
            dims,
            sc,
            [*columns[l], *crossing],
            [blocks(SIB * (levels - 1 - l) + 1)],
            flops=16 * (levels - 1 - l) * unit,
        )
        return lax.psum(right, "col") if l == 0 else col_sum(right)

    def window_level(k, low, high):
        whole = low == 0 and high == k
        outs = [blocks(SIB * (high - low) + whole)]
        if not whole:
            outs.append(blocks(1, dtype=jnp.float32))
        return call(
            functools.partial(window_column, k, low, high),
            dims,
            sc,
            rights[low : high + whole] + flat(solved) + ([wide] if k else []) + ([pivot] if whole else []),
            outs,
            scratch=[pltpu.VMEM((SIB * k, size, size), bf16)] if k else [],
            flops=SIB * (high - low) * (SIB * k - 2) * unit,
        )

    columns, rights, solved = [], [], []
    crossing = [own[0]] + [swap(own[s], "col", s) for s in range(1, SIB)]
    columns.append(row_pieces(top_level(0)))
    rights.append(later_products(0))
    wide = col_pieces(own[SIB])
    pivs = row_pieces(pivot_inverse[:, 0].astype(bf16))
    (pivot,) = call(functools.partial(own_pivots, levels), dims, sc, pivs, [blocks(levels)])
    columns, wide, crossing, pivot = fence((columns, wide, crossing, pivot))
    columns.append(row_pieces(top_level(1)))
    rights.append(later_products(1))
    columns.append(row_pieces(top_level(2)))
    rights.append(later_products(2))
    columns.append(row_pieces(top_level(3)))
    solved.append(row_pieces(window_level(0, 0, 0)[0]))
    columns, crossing, late_pivot = fence((columns, crossing, pivot))
    (top_sum,) = call(
        functools.partial(cross_product, 3, levels), dims, sc, [*columns[3], *crossing], [blocks(1)], flops=4 * unit
    )
    top_sum = col_sum(top_sum)
    starts = [(0, 0, 0, True)]
    for k in range(1, levels - 1):
        pivot = pivot if k < levels - 2 else late_pivot
        solved.append(row_pieces(window_level(k, 0, k)[0]))
        starts.append((k, 0, SIB * k, True))
    k = levels - 1
    early, early_share = window_level(k, 0, k - 1)
    late, late_share = window_level(k, k - 1, k)
    (corner,) = call(
        functools.partial(pivot_block, k), dims, sc, [pivot, top_sum, early_share, late_share], [blocks(1)]
    )
    solved.append(row_pieces(early))
    starts.append((k, 0, SIB * (k - 1), False))
    solved.append(row_pieces(late))
    starts.append((k, k - 1, SIB, False))
    solved.append([swap(corner, "row", d) if d else corner for d in range(SIB)])
    starts.append((k, 0, 0, True))

    packed = call(
        functools.partial(pack_rows, levels),
        dims,
        sc,
        flat(columns),
        [blocks(levels)] * SIB,
        scratch=[pltpu.SemaphoreType.DMA((levels, SIB))],
        hbm=tuple(range(SIB * levels)),
    )
    rows = [packed[0]] + [swap(packed[s], "col", s) for s in range(1, SIB)]
    (out,) = call(
        functools.partial(place, starts),
        dims,
        sc,
        rows + flat(solved),
        [blocks(total // SIB, levels)],
    )
    return out[:, None, :, None]


def solution(mesh):
    in_specs = (
        P("pole", "row", None, "col", None, None),
        P("pole", "row", None, "col", None, None),
        P("pole", "row", None, None),
        P(),
        P(),
        P(),
    )
    out_specs = P("pole", "row", None, "col", None, None)
    square = mesh.shape["row"] == SIB and mesh.shape["col"] == SIB
    return jax.shard_map(
        square_plan if square else per_device, mesh=mesh, in_specs=in_specs, out_specs=out_specs, check_vma=False
    )
```

```python
import functools

import jax
import jax.numpy as jnp
from jax import lax
from jax.experimental import pallas as pl
from jax.experimental.pallas import tpu as pltpu
from jax.sharding import PartitionSpec as P

SIB = 4


def from_root(x, axis, root):
    mine = lax.axis_index(axis) == root
    return lax.psum(jnp.where(mine, x, jnp.zeros_like(x)), axis)


def per_device(top_inverse, upper_factor, pivot_inverse, widths, order, pattern):
    row_count = lax.axis_size("row")
    col_count = lax.axis_size("col")
    row_rank = lax.axis_index("row")
    col_rank = lax.axis_index("col")
    tile_size = top_inverse.shape[-1]
    total_nodes = widths.shape[0]
    window = order.shape[0]
    row_blocks = total_nodes // row_count
    col_blocks = total_nodes // col_count
    row_span = row_count // col_count
    factor = upper_factor[:, 0, :, 0]
    pivots = pivot_inverse[:, 0]
    live_rows = (
        lax.broadcasted_iota(jnp.int32, (total_nodes, tile_size), 1) < widths[:, None]
    ).astype(jnp.bfloat16)
    row_nodes = jnp.arange(row_blocks, dtype=jnp.int32) * row_count + row_rank
    col_nodes = jnp.arange(col_blocks, dtype=jnp.int32) * col_count + col_rank
    blocks_held = jnp.zeros((row_blocks, col_blocks, tile_size, tile_size), jnp.bfloat16)
    blocks_held = blocks_held.at[window // row_count :, window // col_count :].set(
        top_inverse[:, 0, :, 0]
    )
    members = SIB

    def fetch(node_id):
        local_rows = lax.dynamic_index_in_dim(factor, node_id // row_count, 0, keepdims=False)
        return from_root(local_rows, "row", node_id % row_count)

    def panel(node_id):
        received = fetch(node_id)
        present = pattern[col_nodes, node_id].astype(jnp.bfloat16)
        keep_mask = (
            present[:, None, None]
            * live_rows[col_nodes][:, None, :]
            * live_rows[node_id][None, :, None]
        )
        return received * keep_mask

    def step(position, blocks_held):
        node_ids = lax.dynamic_slice_in_dim(order, position * members, members)
        node_list = [node_ids[member] for member in range(members)]
        panels = jnp.stack([panel(node_id) for node_id in node_list])
        partial_value = jnp.einsum(
            "abpq,ibsq->iaps", blocks_held, panels, preferred_element_type=jnp.float32
        )
        summed = lax.psum_scatter(
            partial_value.astype(jnp.bfloat16), "col", scatter_dimension=2, tiled=True
        ).astype(jnp.float32)
        row_share = (-summed).astype(jnp.bfloat16)
        column_new = lax.all_gather(row_share, "col", axis=2, tiled=True)
        present = jnp.transpose(pattern[row_nodes][:, node_ids]).astype(jnp.bfloat16)
        node_live = live_rows[node_ids]
        column_mask = (
            present[:, :, None, None]
            * live_rows[row_nodes][None, :, :, None]
            * node_live[:, None, None, :]
        )
        column_new = column_new * column_mask
        for member, node_id in enumerate(node_list):
            column_at = node_id // col_count
            current = lax.dynamic_slice_in_dim(blocks_held, column_at, 1, 1)
            update = jnp.where(
                col_rank == node_id % col_count, column_new[member][:, None], current
            )
            blocks_held = lax.dynamic_update_slice_in_dim(blocks_held, update, column_at, 1)
        arrived = []
        for offset in range(row_span):
            arrived.append(from_root(column_new, "row", col_rank + offset * col_count))
        mirror = jnp.stack(arrived, 2).reshape(members, row_blocks * row_span, tile_size, tile_size)
        pivot_part = jnp.einsum(
            "ibsq,ibqt->ist", panels, mirror, preferred_element_type=jnp.float32
        )
        pivot_total = lax.psum(pivot_part.astype(jnp.bfloat16), "col").astype(jnp.float32)
        for member, node_id in enumerate(node_list):
            row_at = node_id // row_count
            column_at = node_id // col_count
            on_row = row_rank == node_id % row_count
            on_col = col_rank == node_id % col_count
            current = lax.dynamic_slice_in_dim(blocks_held, row_at, 1, 0)
            flipped = jnp.swapaxes(mirror[member], 1, 2)[None]
            update = jnp.where(on_row, flipped, current)
            own_pivot = lax.dynamic_index_in_dim(pivots, row_at, 0, keepdims=False)
            corner_mask = node_live[member][:, None].astype(jnp.float32) * node_live[member][
                None, :
            ].astype(jnp.float32)
            corner = ((own_pivot - pivot_total[member]) * corner_mask).astype(jnp.bfloat16)
            update = update.at[0, column_at].set(
                jnp.where(on_row & on_col, corner, update[0, column_at])
            )
            blocks_held = lax.dynamic_update_slice_in_dim(blocks_held, update, row_at, 0)
        return blocks_held

    blocks_held = lax.fori_loop(0, window // members, step, blocks_held)
    return blocks_held[:, : window // col_count][:, None, :, None]


VMEM_BYTES = 50 * 1024 * 1024
ORD = 2


def dot_nt(a, b):
    return lax.dot_general(a, b, (((1,), (1,)), ((), ())), preferred_element_type=jnp.float32)


def dot_nn(a, b):
    return jnp.dot(a, b, preferred_element_type=jnp.float32)


class Facts:
    def __init__(self, sc, window, total):
        self.sc, self.window = sc, window
        self.pat_at = ORD + window
        self.wid_at = self.pat_at + window * total
        self.r, self.c = sc[0], sc[1]

    def node(self, level, member):
        return self.sc[ORD + level * SIB + member]

    def pat(self, row, col):
        return self.sc[self.pat_at + row * self.window + col]

    def width(self, node):
        return self.sc[self.wid_at + node]


def keep(x, rows, cols):
    at_row = lax.broadcasted_iota(jnp.int32, x.shape, 0)
    at_col = lax.broadcasted_iota(jnp.int32, x.shape, 1)
    return jnp.where((at_row < rows) & (at_col < cols), x, 0.0)


def call(body, dims, sc, inputs, outs, scratch=(), hbm=(), flops=0):
    specs = [pl.BlockSpec(memory_space=pltpu.SMEM)]
    for at in range(len(inputs)):
        specs.append(pl.BlockSpec(memory_space=pl.ANY if at in hbm else pltpu.VMEM))
    moved = sum(x.size * x.dtype.itemsize for x in list(inputs) + list(outs))

    def kernel(sc_ref, *refs):
        body(Facts(sc_ref, *dims), *refs)

    return pl.pallas_call(
        kernel,
        out_shape=list(outs),
        in_specs=specs,
        out_specs=[pl.BlockSpec(memory_space=pltpu.VMEM)] * len(outs),
        scratch_shapes=list(scratch),
        compiler_params=pltpu.CompilerParams(vmem_limit_bytes=VMEM_BYTES),
        cost_estimate=pl.CostEstimate(flops=flops, bytes_accessed=moved, transcendentals=0),
    )(sc, *inputs)


def swap(x, axis, d):
    count = lax.axis_size(axis)
    return lax.ppermute(x, axis, [(i, i ^ d) for i in range(count)])


def row_pieces(x):
    far = swap(x, "row", 2)
    return [x, swap(x, "row", 1), far, swap(far, "row", 1)]


def col_pieces(x):
    rank = lax.axis_index("col")
    last = SIB - 1
    up, down = [x], [x]
    for hop in range(1, SIB):
        down.append(lax.ppermute(down[-1], "col", [(i + 1, i) for i in range(SIB - hop)]))
        up.append(lax.ppermute(up[-1], "col", [(i, i + 1) for i in range(hop - 1, last)]))
    one = jnp.where(rank % 2 == 0, down[1], up[1])
    two = jnp.where(rank < 2, down[2], up[2])
    lower = jnp.where(rank == 0, down[3], down[1])
    upper = jnp.where(rank == last, up[3], up[1])
    return jnp.stack([x, one, two, jnp.where(rank < 2, lower, upper)])


def col_sum(x):
    last = SIB - 1
    at_end = (lax.axis_index("col") == 0) | (lax.axis_index("col") == last)

    def add(a, b):
        return (a.astype(jnp.float32) + b.astype(jnp.float32)).astype(jnp.bfloat16)

    half = add(x, lax.ppermute(x, "col", [(0, 1), (last, last - 1)]))
    full = add(half, lax.ppermute(half, "col", [(1, 2), (2, 1)]))
    return jnp.where(at_end, lax.ppermute(full, "col", [(1, 0), (last - 1, last)]), full)


def top_product(first, f, h, u0, u1, u2, u3, out, ubuf, lbuf, sems):
    pieces = (u0, u1, u2, u3)
    size = h.shape[-1]
    depth = h.shape[1]
    count = out.shape[1]
    for m in range(count):
        node = f.node(first, m)
        for d in range(SIB):

            @pl.when((node % SIB) ^ f.r == d)
            def _():
                pltpu.make_async_copy(pieces[d].at[node // SIB], ubuf.at[m], sems.at[m]).start()

    for m in range(count):
        node = f.node(first, m)
        pltpu.make_async_copy(u0.at[0], ubuf.at[m], sems.at[m]).wait()
        for b in range(depth):
            at = f.window + b * SIB + f.c
            reach = jnp.where(f.pat(at, node) > 0, f.width(at), 0)
            kept = keep(ubuf[m, b].astype(jnp.float32), size, reach)
            lbuf[m, :, b * size : (b + 1) * size] = kept.astype(jnp.bfloat16)
    for a in range(h.shape[0]):
        rows = jnp.concatenate([h[a, b] for b in range(depth)], axis=1)
        for m in range(count):
            out[a, m] = dot_nt(rows, lbuf[m]).astype(jnp.bfloat16)


def own_blocks(levels, f, *refs):
    tops, wins = refs[0:4], refs[4:8]
    by_slice, by_level, sems = refs[8:12], refs[12], refs[13]
    near = wins[0].shape[1]
    for wait in (False, True):
        for k in range(levels):
            node = f.node(k, f.r)
            at = node // SIB
            source = (node % SIB) ^ f.r
            for d in range(SIB):
                copies = [
                    pltpu.make_async_copy(tops[d].at[at, f.c ^ s], by_slice[s].at[k], sems.at[k, s])
                    for s in range(SIB)
                ]
                if k:
                    room = by_level.at[pl.ds((k - 1) * near, near)]
                    copies.append(pltpu.make_async_copy(wins[d].at[at], room, sems.at[k, SIB]))

                @pl.when(source == d)
                def _():
                    for copy in copies:
                        if wait:
                            copy.wait()
                        else:
                            copy.start()


def own_pivots(levels, f, p0, p1, p2, p3, out):
    pieces = (p0, p1, p2, p3)
    for k in range(levels):
        node = f.node(k, f.r)
        for d in range(SIB):

            @pl.when((node % SIB) ^ f.r == d)
            def _():
                out[k] = pieces[d][node // SIB]


def wide_at(level):
    return (level - 1) * SIB


def top_column(level, f, *refs):
    ys = refs[0:SIB]
    earlier = refs[SIB : SIB + SIB * level]
    out = refs[-1]
    node = f.node(level, f.r)
    acc = [y[...].astype(jnp.float32) for y in ys]
    if level:
        lw = refs[-2]
        for j in range(level):
            for d in range(SIB):
                at = f.node(j, f.r ^ d)
                block = lw[(at % SIB) ^ f.c, wide_at(level) + at // SIB]
                block = jnp.where(f.pat(at, node) > 0, block, jnp.zeros_like(block))
                for e in range(SIB):
                    acc[e] += dot_nt(earlier[j * SIB + d][d ^ e], block)
    for e in range(SIB):
        row = f.window + f.c * SIB + (f.r ^ e)
        reach = jnp.where(f.pat(row, node) > 0, f.width(row), 0)
        out[e] = keep(-acc[e], reach, f.width(node)).astype(jnp.bfloat16)


def cross_product(level, levels, f, *refs):
    xs, ts, out = refs[0:4], refs[4:8], refs[8]
    turn = f.c ^ f.r
    for k in range(level, levels):
        node = f.node(k, f.r)
        parts = []
        for s in range(SIB):
            row = f.window + f.c * SIB + (f.c ^ s)
            block = ts[s][k]
            parts.append(jnp.where(f.pat(row, node) > 0, block, jnp.zeros_like(block)))
        left = jnp.concatenate(parts, axis=1)
        for d in range(SIB if k > level else 1):
            right = jnp.concatenate([xs[d][turn ^ (s ^ d)] for s in range(SIB)], axis=0)
            at = (k - level - 1) * SIB + d if k > level else (levels - 1 - level) * SIB
            out[at] = dot_nn(left, right).astype(jnp.bfloat16)


def window_column(k, low, high, f, *refs):
    whole = low == 0 and high == k
    count = high - low + whole
    vs = refs[0:count]
    zs = [refs[count + SIB * i : count + SIB * (i + 1)] for i in range(k)]
    at = count + SIB * k
    node = f.node(k, f.r)
    width = f.width(node)
    if k:
        lw, ub = refs[at], refs[-1]
        at += 1
    if whole:
        piv, out = refs[at], refs[at + 1]
        total = vs[-1][vs[-1].shape[0] - 1].astype(jnp.float32)
    else:
        out, share = refs[at], refs[at + 1]
        total = jnp.zeros(ub.shape[1:], jnp.float32)
    for i in range(k):
        for d in range(SIB):
            at = f.node(i, f.r ^ d)
            block = lw[(at % SIB) ^ f.c, wide_at(k) + at // SIB]
            ub[i * SIB + d] = jnp.where(f.pat(at, node) > 0, block, jnp.zeros_like(block))
    for j in range(low, high):
        for d in range(SIB):
            acc = vs[j - low][(k - j - 1) * SIB + d].astype(jnp.float32)
            for i in range(k):
                for e in range(SIB):
                    left = ub[i * SIB + e]
                    if i > j:
                        acc += dot_nn(left, zs[i][e][j * SIB + (d ^ e)])
                    elif i < j:
                        acc += dot_nt(left, zs[j][d][i * SIB + (d ^ e)])
                    elif d == e:
                        acc += dot_nt(left, zs[j][d][j * SIB])
            at = f.node(j, f.r ^ d)
            reach = jnp.where(f.pat(at, node) > 0, f.width(at), 0)
            block = keep(-acc, width, reach).astype(jnp.bfloat16)
            out[(j - low) * SIB + d] = block
            total += dot_nt(ub[j * SIB + d], block)
    if whole:
        corner = piv[k].astype(jnp.float32) - total
        out[k * SIB] = keep(corner, width, width).astype(jnp.bfloat16)
    else:
        share[0] = total


def pivot_block(k, f, piv, top_sum, *refs):
    out = refs[-1]
    total = top_sum[0].astype(jnp.float32)
    for part in refs[:-1]:
        total += part[0]
    width = f.width(f.node(k, f.r))
    out[0] = keep(piv[k].astype(jnp.float32) - total, width, width).astype(jnp.bfloat16)


def pack_rows(levels, f, *refs):
    xs, outs, sems = refs[: SIB * levels], refs[SIB * levels : SIB * levels + SIB], refs[-1]
    for wait in (False, True):
        for l in range(levels):
            for d in range(SIB):
                node = f.node(l, f.r ^ d)
                for s in range(SIB):

                    @pl.when((node % SIB) ^ f.c == s)
                    def _():
                        copy = pltpu.make_async_copy(
                            xs[l * SIB + d].at[d], outs[s].at[node // SIB], sems.at[l, d]
                        )
                        if wait:
                            copy.wait()
                        else:
                            copy.start()


def place(starts, f, *refs):
    rows, out = refs[0:SIB], refs[-1]
    top = out.shape[0] // 2
    for s in range(SIB):
        out[top + (f.c ^ s)] = rows[s][...]
    out[0:top] = jnp.zeros_like(out[0:top])
    for at, (k, low, count, corner) in enumerate(starts):
        for d in range(SIB):
            z = refs[SIB + at * SIB + d]
            node = f.node(k, f.r ^ d)
            on_row, on_col = node % SIB == f.r, node % SIB == f.c
            if count:

                @pl.loop(0, count)
                def _(at):
                    other = f.node(low + at // SIB, f.r ^ d ^ (at % SIB))

                    @pl.when(on_row & (other % SIB == f.c))
                    def _():
                        out[node // SIB, other // SIB] = z[at]

                    @pl.when(on_col & (other % SIB == f.r))
                    def _():
                        out[other // SIB, node // SIB] = z[at].T

            if corner:

                @pl.when(on_row & on_col)
                def _():
                    out[node // SIB, node // SIB] = z[count]


def square_plan(top_inverse, upper_factor, pivot_inverse, widths, order, pattern):
    row_rank = lax.axis_index("row")
    col_rank = lax.axis_index("col")
    size = top_inverse.shape[-1]
    total, window = widths.shape[0], order.shape[0]
    levels = window // SIB
    near = window // SIB
    bf16 = jnp.bfloat16
    dims = (window, total)

    def blocks(*lead, dtype=bf16):
        return jax.ShapeDtypeStruct((*lead, size, size), dtype)

    unit = 2 * size**3
    ranks = jnp.stack([row_rank, col_rank]).astype(jnp.int32)
    sc = jnp.concatenate([ranks, order, pattern.reshape(-1), widths])
    known = top_inverse[:, 0, :, 0]
    factor = upper_factor[:, 0, :, 0]
    tops = row_pieces(factor[:, near:])
    groups = [(0, 1), (1, levels - 1)]
    parts = [
        call(
            functools.partial(top_product, first),
            dims,
            sc,
            [known, *tops],
            [blocks(levels, SIB * count)],
            scratch=[
                pltpu.VMEM((SIB * count, levels, size, size), bf16),
                pltpu.VMEM((SIB * count, size, levels * size), bf16),
                pltpu.SemaphoreType.DMA((SIB * count,)),
            ],
            hbm=(1, 2, 3, 4),
            flops=64 * count * unit,
        )[0]
        for first, count in groups
    ]
    fence = lax.optimization_barrier
    sums = []
    for part, (_, count) in zip(parts, groups):
        total_part = lax.psum_scatter(part, "col", scatter_dimension=0)
        sums += [(total_part, at * SIB) for at in range(count)]
    window_factor, _ = fence((factor[:, :near], parts))
    wins = row_pieces(window_factor)
    own = call(
        functools.partial(own_blocks, levels),
        dims,
        sc,
        [*tops, *wins],
        [blocks(levels)] * SIB + [blocks((levels - 1) * near)],
        scratch=[pltpu.SemaphoreType.DMA((levels, SIB + 1))],
        hbm=tuple(range(8)),
    )
    own = list(own)

    def flat(lists):
        return [x for xs in lists for x in xs]

    def top_level(l):
        ys = []
        for d in range(SIB):
            share = lax.dynamic_index_in_dim(sums[l][0], sums[l][1] + (row_rank ^ d), 0, keepdims=False)
            ys.append(swap(share, "row", d) if d else share)
        return call(
            functools.partial(top_column, l),
            dims,
            sc,
            ys + flat(columns) + ([wide] if l else []),
            [blocks(SIB)],
            flops=16 * l * unit,
        )[0]

    def later_products(l):
        (right,) = call(
            functools.partial(cross_product, l, levels),
            dims,
            sc,
            [*columns[l], *crossing],
            [blocks(SIB * (levels - 1 - l) + 1)],
            flops=16 * (levels - 1 - l) * unit,
        )
        return right

    def window_level(k, low, high):
        whole = low == 0 and high == k
        outs = [blocks(SIB * (high - low) + whole)]
        if not whole:
            outs.append(blocks(1, dtype=jnp.float32))
        return call(
            functools.partial(window_column, k, low, high),
            dims,
            sc,
            rights[low : high + whole] + flat(solved) + ([wide] if k else []) + ([pivot] if whole else []),
            outs,
            scratch=[pltpu.VMEM((SIB * k, size, size), bf16)] if k else [],
            flops=SIB * (high - low) * (SIB * k - 2) * unit,
        )

    columns, rights, solved = [], [], []
    crossing = [own[0]] + [swap(own[s], "col", s) for s in range(1, SIB)]
    columns.append(row_pieces(top_level(0)))
    pivs = row_pieces(pivot_inverse[:, 0].astype(bf16))
    (pivot,) = call(functools.partial(own_pivots, levels), dims, sc, pivs, [blocks(levels)])
    columns, crossing, pivot, own = fence((columns, crossing, pivot, own))
    right, own = fence((later_products(0), own))
    rights.append(lax.psum(right, "col"))
    wide = col_pieces(own[SIB])
    columns.append(row_pieces(top_level(1)))
    rights.append(col_sum(later_products(1)))
    columns.append(row_pieces(top_level(2)))
    rights.append(col_sum(later_products(2)))
    columns.append(row_pieces(top_level(3)))
    columns, crossing, pivot = fence((columns, crossing, pivot))
    solved.append(row_pieces(window_level(0, 0, 0)[0]))
    (top_sum,) = call(
        functools.partial(cross_product, 3, levels), dims, sc, [*columns[3], *crossing], [blocks(1)], flops=4 * unit
    )
    top_sum = col_sum(top_sum)
    starts = [(0, 0, 0, True)]
    for k in range(1, levels - 1):
        solved.append(row_pieces(window_level(k, 0, k)[0]))
        starts.append((k, 0, SIB * k, True))
    k = levels - 1
    early, early_share = window_level(k, 0, k - 1)
    late, late_share = window_level(k, k - 1, k)
    (corner,) = call(
        functools.partial(pivot_block, k), dims, sc, [pivot, top_sum, early_share, late_share], [blocks(1)]
    )
    solved.append(row_pieces(early))
    starts.append((k, 0, SIB * (k - 1), False))
    solved.append(row_pieces(late))
    starts.append((k, k - 1, SIB, False))
    solved.append([swap(corner, "row", d) if d else corner for d in range(SIB)])
    starts.append((k, 0, 0, True))

    packed = call(
        functools.partial(pack_rows, levels),
        dims,
        sc,
        flat(columns),
        [blocks(levels)] * SIB,
        scratch=[pltpu.SemaphoreType.DMA((levels, SIB))],
        hbm=tuple(range(SIB * levels)),
    )
    rows = [packed[0]] + [swap(packed[s], "col", s) for s in range(1, SIB)]
    (out,) = call(
        functools.partial(place, starts),
        dims,
        sc,
        rows + flat(solved),
        [blocks(total // SIB, levels)],
    )
    return out[:, None, :, None]


def solution(mesh):
    in_specs = (
        P("pole", "row", None, "col", None, None),
        P("pole", "row", None, "col", None, None),
        P("pole", "row", None, None),
        P(),
        P(),
        P(),
    )
    out_specs = P("pole", "row", None, "col", None, None)
    square = mesh.shape["row"] == SIB and mesh.shape["col"] == SIB
    return jax.shard_map(
        square_plan if square else per_device, mesh=mesh, in_specs=in_specs, out_specs=out_specs, check_vma=False
    )
```

```python
import functools

import jax
import jax.numpy as jnp
from jax import lax
from jax.experimental import pallas as pl
from jax.experimental.pallas import tpu as pltpu
from jax.sharding import PartitionSpec as P

SIB = 4


def from_root(x, axis, root):
    mine = lax.axis_index(axis) == root
    return lax.psum(jnp.where(mine, x, jnp.zeros_like(x)), axis)


def per_device(top_inverse, upper_factor, pivot_inverse, widths, order, pattern):
    row_count = lax.axis_size("row")
    col_count = lax.axis_size("col")
    row_rank = lax.axis_index("row")
    col_rank = lax.axis_index("col")
    tile_size = top_inverse.shape[-1]
    total_nodes = widths.shape[0]
    window = order.shape[0]
    row_blocks = total_nodes // row_count
    col_blocks = total_nodes // col_count
    row_span = row_count // col_count
    factor = upper_factor[:, 0, :, 0]
    pivots = pivot_inverse[:, 0]
    live_rows = (
        lax.broadcasted_iota(jnp.int32, (total_nodes, tile_size), 1) < widths[:, None]
    ).astype(jnp.bfloat16)
    row_nodes = jnp.arange(row_blocks, dtype=jnp.int32) * row_count + row_rank
    col_nodes = jnp.arange(col_blocks, dtype=jnp.int32) * col_count + col_rank
    blocks_held = jnp.zeros((row_blocks, col_blocks, tile_size, tile_size), jnp.bfloat16)
    blocks_held = blocks_held.at[window // row_count :, window // col_count :].set(
        top_inverse[:, 0, :, 0]
    )
    members = SIB

    def fetch(node_id):
        local_rows = lax.dynamic_index_in_dim(factor, node_id // row_count, 0, keepdims=False)
        return from_root(local_rows, "row", node_id % row_count)

    def panel(node_id):
        received = fetch(node_id)
        present = pattern[col_nodes, node_id].astype(jnp.bfloat16)
        keep_mask = (
            present[:, None, None]
            * live_rows[col_nodes][:, None, :]
            * live_rows[node_id][None, :, None]
        )
        return received * keep_mask

    def step(position, blocks_held):
        node_ids = lax.dynamic_slice_in_dim(order, position * members, members)
        node_list = [node_ids[member] for member in range(members)]
        panels = jnp.stack([panel(node_id) for node_id in node_list])
        partial_value = jnp.einsum(
            "abpq,ibsq->iaps", blocks_held, panels, preferred_element_type=jnp.float32
        )
        summed = lax.psum_scatter(
            partial_value.astype(jnp.bfloat16), "col", scatter_dimension=2, tiled=True
        ).astype(jnp.float32)
        row_share = (-summed).astype(jnp.bfloat16)
        column_new = lax.all_gather(row_share, "col", axis=2, tiled=True)
        present = jnp.transpose(pattern[row_nodes][:, node_ids]).astype(jnp.bfloat16)
        node_live = live_rows[node_ids]
        column_mask = (
            present[:, :, None, None]
            * live_rows[row_nodes][None, :, :, None]
            * node_live[:, None, None, :]
        )
        column_new = column_new * column_mask
        for member, node_id in enumerate(node_list):
            column_at = node_id // col_count
            current = lax.dynamic_slice_in_dim(blocks_held, column_at, 1, 1)
            update = jnp.where(
                col_rank == node_id % col_count, column_new[member][:, None], current
            )
            blocks_held = lax.dynamic_update_slice_in_dim(blocks_held, update, column_at, 1)
        arrived = []
        for offset in range(row_span):
            arrived.append(from_root(column_new, "row", col_rank + offset * col_count))
        mirror = jnp.stack(arrived, 2).reshape(members, row_blocks * row_span, tile_size, tile_size)
        pivot_part = jnp.einsum(
            "ibsq,ibqt->ist", panels, mirror, preferred_element_type=jnp.float32
        )
        pivot_total = lax.psum(pivot_part.astype(jnp.bfloat16), "col").astype(jnp.float32)
        for member, node_id in enumerate(node_list):
            row_at = node_id // row_count
            column_at = node_id // col_count
            on_row = row_rank == node_id % row_count
            on_col = col_rank == node_id % col_count
            current = lax.dynamic_slice_in_dim(blocks_held, row_at, 1, 0)
            flipped = jnp.swapaxes(mirror[member], 1, 2)[None]
            update = jnp.where(on_row, flipped, current)
            own_pivot = lax.dynamic_index_in_dim(pivots, row_at, 0, keepdims=False)
            corner_mask = node_live[member][:, None].astype(jnp.float32) * node_live[member][
                None, :
            ].astype(jnp.float32)
            corner = ((own_pivot - pivot_total[member]) * corner_mask).astype(jnp.bfloat16)
            update = update.at[0, column_at].set(
                jnp.where(on_row & on_col, corner, update[0, column_at])
            )
            blocks_held = lax.dynamic_update_slice_in_dim(blocks_held, update, row_at, 0)
        return blocks_held

    blocks_held = lax.fori_loop(0, window // members, step, blocks_held)
    return blocks_held[:, : window // col_count][:, None, :, None]


VMEM_BYTES = 50 * 1024 * 1024
ORD = 2


def dot_nt(a, b):
    return lax.dot_general(a, b, (((1,), (1,)), ((), ())), preferred_element_type=jnp.float32)


def dot_nn(a, b):
    return jnp.dot(a, b, preferred_element_type=jnp.float32)


class Facts:
    def __init__(self, sc, window, total):
        self.sc, self.window = sc, window
        self.pat_at = ORD + window
        self.wid_at = self.pat_at + window * total
        self.r, self.c = sc[0], sc[1]

    def node(self, level, member):
        return self.sc[ORD + level * SIB + member]

    def pat(self, row, col):
        return self.sc[self.pat_at + row * self.window + col]

    def width(self, node):
        return self.sc[self.wid_at + node]


def keep(x, rows, cols):
    at_row = lax.broadcasted_iota(jnp.int32, x.shape, 0)
    at_col = lax.broadcasted_iota(jnp.int32, x.shape, 1)
    return jnp.where((at_row < rows) & (at_col < cols), x, 0.0)


def call(body, dims, sc, inputs, outs, scratch=(), hbm=(), flops=0):
    specs = [pl.BlockSpec(memory_space=pltpu.SMEM)]
    for at in range(len(inputs)):
        specs.append(pl.BlockSpec(memory_space=pl.ANY if at in hbm else pltpu.VMEM))
    moved = sum(x.size * x.dtype.itemsize for x in list(inputs) + list(outs))

    def kernel(sc_ref, *refs):
        body(Facts(sc_ref, *dims), *refs)

    return pl.pallas_call(
        kernel,
        out_shape=list(outs),
        in_specs=specs,
        out_specs=[pl.BlockSpec(memory_space=pltpu.VMEM)] * len(outs),
        scratch_shapes=list(scratch),
        compiler_params=pltpu.CompilerParams(vmem_limit_bytes=VMEM_BYTES),
        cost_estimate=pl.CostEstimate(flops=flops, bytes_accessed=moved, transcendentals=0),
    )(sc, *inputs)


def swap(x, axis, d):
    count = lax.axis_size(axis)
    return lax.ppermute(x, axis, [(i, i ^ d) for i in range(count)])


def row_pieces(x):
    far = swap(x, "row", 2)
    return [x, swap(x, "row", 1), far, swap(far, "row", 1)]


def col_hop(hop, down, up):
    last = SIB - 1
    return (
        lax.ppermute(down, "col", [(i + 1, i) for i in range(SIB - hop)]),
        lax.ppermute(up, "col", [(i, i + 1) for i in range(hop - 1, last)]),
    )


def col_pieces(x, first):
    rank = lax.axis_index("col")
    last = SIB - 1
    down, up = [x, first[0]], [x, first[1]]
    for hop in range(2, SIB):
        next_down, next_up = col_hop(hop, down[-1], up[-1])
        down.append(next_down)
        up.append(next_up)
    one = jnp.where(rank % 2 == 0, down[1], up[1])
    two = jnp.where(rank < 2, down[2], up[2])
    lower = jnp.where(rank == 0, down[3], down[1])
    upper = jnp.where(rank == last, up[3], up[1])
    return jnp.stack([x, one, two, jnp.where(rank < 2, lower, upper)])


def col_sum(x):
    last = SIB - 1
    at_end = (lax.axis_index("col") == 0) | (lax.axis_index("col") == last)

    def add(a, b):
        return (a.astype(jnp.float32) + b.astype(jnp.float32)).astype(jnp.bfloat16)

    half = add(x, lax.ppermute(x, "col", [(0, 1), (last, last - 1)]))
    full = add(half, lax.ppermute(half, "col", [(1, 2), (2, 1)]))
    return jnp.where(at_end, lax.ppermute(full, "col", [(1, 0), (last - 1, last)]), full)


def top_product(first, f, h, u0, u1, u2, u3, out, ubuf, lbuf, sems):
    pieces = (u0, u1, u2, u3)
    size = h.shape[-1]
    depth = h.shape[1]
    count = out.shape[1]
    for m in range(count):
        node = f.node(first, m)
        for d in range(SIB):

            @pl.when((node % SIB) ^ f.r == d)
            def _():
                pltpu.make_async_copy(pieces[d].at[node // SIB], ubuf.at[m], sems.at[m]).start()

    for m in range(count):
        node = f.node(first, m)
        pltpu.make_async_copy(u0.at[0], ubuf.at[m], sems.at[m]).wait()
        for b in range(depth):
            at = f.window + b * SIB + f.c
            reach = jnp.where(f.pat(at, node) > 0, f.width(at), 0)
            kept = keep(ubuf[m, b].astype(jnp.float32), size, reach)
            lbuf[m, :, b * size : (b + 1) * size] = kept.astype(jnp.bfloat16)
    for a in range(h.shape[0]):
        rows = jnp.concatenate([h[a, b] for b in range(depth)], axis=1)
        for m in range(count):
            out[a, m] = dot_nt(rows, lbuf[m]).astype(jnp.bfloat16)


def own_blocks(levels, f, *refs):
    tops, wins = refs[0:4], refs[4:8]
    by_slice, by_level, sems = refs[8:12], refs[12], refs[13]
    near = wins[0].shape[1]
    for wait in (False, True):
        for k in range(levels):
            node = f.node(k, f.r)
            at = node // SIB
            source = (node % SIB) ^ f.r
            for d in range(SIB):
                copies = [
                    pltpu.make_async_copy(tops[d].at[at, f.c ^ s], by_slice[s].at[k], sems.at[k, s])
                    for s in range(SIB)
                ]
                if k:
                    room = by_level.at[pl.ds((k - 1) * near, near)]
                    copies.append(pltpu.make_async_copy(wins[d].at[at], room, sems.at[k, SIB]))

                @pl.when(source == d)
                def _():
                    for copy in copies:
                        if wait:
                            copy.wait()
                        else:
                            copy.start()


def own_pivots(levels, f, p0, p1, p2, p3, out):
    pieces = (p0, p1, p2, p3)
    for k in range(levels):
        node = f.node(k, f.r)
        for d in range(SIB):

            @pl.when((node % SIB) ^ f.r == d)
            def _():
                out[k] = pieces[d][node // SIB]


def wide_at(level):
    return (level - 1) * SIB


def top_column(level, f, *refs):
    ys = refs[0:SIB]
    earlier = refs[SIB : SIB + SIB * level]
    out = refs[-1]
    node = f.node(level, f.r)
    acc = [y[...].astype(jnp.float32) for y in ys]
    if level:
        lw = refs[-2]
        for j in range(level):
            for d in range(SIB):
                at = f.node(j, f.r ^ d)
                block = lw[(at % SIB) ^ f.c, wide_at(level) + at // SIB]
                block = jnp.where(f.pat(at, node) > 0, block, jnp.zeros_like(block))
                for e in range(SIB):
                    acc[e] += dot_nt(earlier[j * SIB + d][d ^ e], block)
    for e in range(SIB):
        row = f.window + f.c * SIB + (f.r ^ e)
        reach = jnp.where(f.pat(row, node) > 0, f.width(row), 0)
        out[e] = keep(-acc[e], reach, f.width(node)).astype(jnp.bfloat16)


def cross_product(level, levels, f, *refs):
    xs, ts, out = refs[0:4], refs[4:8], refs[8]
    turn = f.c ^ f.r
    for k in range(level, levels):
        node = f.node(k, f.r)
        parts = []
        for s in range(SIB):
            row = f.window + f.c * SIB + (f.c ^ s)
            block = ts[s][k]
            parts.append(jnp.where(f.pat(row, node) > 0, block, jnp.zeros_like(block)))
        left = jnp.concatenate(parts, axis=1)
        for d in range(SIB if k > level else 1):
            right = jnp.concatenate([xs[d][turn ^ (s ^ d)] for s in range(SIB)], axis=0)
            at = (k - level - 1) * SIB + d if k > level else (levels - 1 - level) * SIB
            out[at] = dot_nn(left, right).astype(jnp.bfloat16)


def window_column(k, low, high, f, *refs):
    whole = low == 0 and high == k
    count = high - low + whole
    vs = refs[0:count]
    zs = [refs[count + SIB * i : count + SIB * (i + 1)] for i in range(k)]
    at = count + SIB * k
    node = f.node(k, f.r)
    width = f.width(node)
    if k:
        lw, ub = refs[at], refs[-1]
        at += 1
    if whole:
        piv, out = refs[at], refs[at + 1]
        total = vs[-1][vs[-1].shape[0] - 1].astype(jnp.float32)
    else:
        out, share = refs[at], refs[at + 1]
        total = jnp.zeros(ub.shape[1:], jnp.float32)
    for i in range(k):
        for d in range(SIB):
            at = f.node(i, f.r ^ d)
            block = lw[(at % SIB) ^ f.c, wide_at(k) + at // SIB]
            ub[i * SIB + d] = jnp.where(f.pat(at, node) > 0, block, jnp.zeros_like(block))
    for j in range(low, high):
        for d in range(SIB):
            acc = vs[j - low][(k - j - 1) * SIB + d].astype(jnp.float32)
            for i in range(k):
                for e in range(SIB):
                    left = ub[i * SIB + e]
                    if i > j:
                        acc += dot_nn(left, zs[i][e][j * SIB + (d ^ e)])
                    elif i < j:
                        acc += dot_nt(left, zs[j][d][i * SIB + (d ^ e)])
                    elif d == e:
                        acc += dot_nt(left, zs[j][d][j * SIB])
            at = f.node(j, f.r ^ d)
            reach = jnp.where(f.pat(at, node) > 0, f.width(at), 0)
            block = keep(-acc, width, reach).astype(jnp.bfloat16)
            out[(j - low) * SIB + d] = block
            total += dot_nt(ub[j * SIB + d], block)
    if whole:
        corner = piv[k].astype(jnp.float32) - total
        out[k * SIB] = keep(corner, width, width).astype(jnp.bfloat16)
    else:
        share[0] = total


def pivot_block(k, f, piv, top_sum, *refs):
    out = refs[-1]
    total = top_sum[0].astype(jnp.float32)
    for part in refs[:-1]:
        total += part[0]
    width = f.width(f.node(k, f.r))
    out[0] = keep(piv[k].astype(jnp.float32) - total, width, width).astype(jnp.bfloat16)


def pack_rows(levels, f, *refs):
    xs, outs, sems = refs[: SIB * levels], refs[SIB * levels : SIB * levels + SIB], refs[-1]
    for wait in (False, True):
        for l in range(levels):
            for d in range(SIB):
                node = f.node(l, f.r ^ d)
                for s in range(SIB):

                    @pl.when((node % SIB) ^ f.c == s)
                    def _():
                        copy = pltpu.make_async_copy(
                            xs[l * SIB + d].at[d], outs[s].at[node // SIB], sems.at[l, d]
                        )
                        if wait:
                            copy.wait()
                        else:
                            copy.start()


def place(starts, f, *refs):
    rows, out = refs[0:SIB], refs[-1]
    top = out.shape[0] // 2
    for s in range(SIB):
        out[top + (f.c ^ s)] = rows[s][...]
    out[0:top] = jnp.zeros_like(out[0:top])
    for at, (k, low, count, corner) in enumerate(starts):
        for d in range(SIB):
            z = refs[SIB + at * SIB + d]
            node = f.node(k, f.r ^ d)
            on_row, on_col = node % SIB == f.r, node % SIB == f.c
            if count:

                @pl.loop(0, count)
                def _(at):
                    other = f.node(low + at // SIB, f.r ^ d ^ (at % SIB))

                    @pl.when(on_row & (other % SIB == f.c))
                    def _():
                        out[node // SIB, other // SIB] = z[at]

                    @pl.when(on_col & (other % SIB == f.r))
                    def _():
                        out[other // SIB, node // SIB] = z[at].T

            if corner:

                @pl.when(on_row & on_col)
                def _():
                    out[node // SIB, node // SIB] = z[count]


def square_plan(top_inverse, upper_factor, pivot_inverse, widths, order, pattern):
    row_rank = lax.axis_index("row")
    col_rank = lax.axis_index("col")
    size = top_inverse.shape[-1]
    total, window = widths.shape[0], order.shape[0]
    levels = window // SIB
    near = window // SIB
    bf16 = jnp.bfloat16
    dims = (window, total)

    def blocks(*lead, dtype=bf16):
        return jax.ShapeDtypeStruct((*lead, size, size), dtype)

    unit = 2 * size**3
    ranks = jnp.stack([row_rank, col_rank]).astype(jnp.int32)
    sc = jnp.concatenate([ranks, order, pattern.reshape(-1), widths])
    known = top_inverse[:, 0, :, 0]
    factor = upper_factor[:, 0, :, 0]
    tops = row_pieces(factor[:, near:])
    groups = [(0, 1), (1, levels - 1)]
    parts = [
        call(
            functools.partial(top_product, first),
            dims,
            sc,
            [known, *tops],
            [blocks(levels, SIB * count)],
            scratch=[
                pltpu.VMEM((SIB * count, levels, size, size), bf16),
                pltpu.VMEM((SIB * count, size, levels * size), bf16),
                pltpu.SemaphoreType.DMA((SIB * count,)),
            ],
            hbm=(1, 2, 3, 4),
            flops=64 * count * unit,
        )[0]
        for first, count in groups
    ]
    fence = lax.optimization_barrier
    sums = []
    for part, (_, count) in zip(parts, groups):
        total_part = lax.psum_scatter(part, "col", scatter_dimension=0)
        sums += [(total_part, at * SIB) for at in range(count)]
    window_factor, _ = fence((factor[:, :near], parts))
    wins = row_pieces(window_factor)
    own = call(
        functools.partial(own_blocks, levels),
        dims,
        sc,
        [*tops, *wins],
        [blocks(levels)] * SIB + [blocks((levels - 1) * near)],
        scratch=[pltpu.SemaphoreType.DMA((levels, SIB + 1))],
        hbm=tuple(range(8)),
    )
    own = list(own)

    def flat(lists):
        return [x for xs in lists for x in xs]

    def top_level(l):
        ys = []
        for d in range(SIB):
            share = lax.dynamic_index_in_dim(sums[l][0], sums[l][1] + (row_rank ^ d), 0, keepdims=False)
            ys.append(swap(share, "row", d) if d else share)
        return call(
            functools.partial(top_column, l),
            dims,
            sc,
            ys + flat(columns) + ([wide] if l else []),
            [blocks(SIB)],
            flops=16 * l * unit,
        )[0]

    def later_products(l):
        (right,) = call(
            functools.partial(cross_product, l, levels),
            dims,
            sc,
            [*columns[l], *crossing],
            [blocks(SIB * (levels - 1 - l) + 1)],
            flops=16 * (levels - 1 - l) * unit,
        )
        return right

    def window_level(k, low, high):
        whole = low == 0 and high == k
        outs = [blocks(SIB * (high - low) + whole)]
        if not whole:
            outs.append(blocks(1, dtype=jnp.float32))
        return call(
            functools.partial(window_column, k, low, high),
            dims,
            sc,
            rights[low : high + whole] + flat(solved) + ([wide] if k else []) + ([pivot] if whole else []),
            outs,
            scratch=[pltpu.VMEM((SIB * k, size, size), bf16)] if k else [],
            flops=SIB * (high - low) * (SIB * k - 2) * unit,
        )

    columns, rights, solved = [], [], []
    crossing = [own[0]] + [swap(own[s], "col", s) for s in range(1, SIB)]
    first = col_hop(1, own[SIB], own[SIB])
    columns.append(row_pieces(top_level(0)))
    pivs = row_pieces(pivot_inverse[:, 0].astype(bf16))
    (pivot,) = call(functools.partial(own_pivots, levels), dims, sc, pivs, [blocks(levels)])
    columns, crossing, pivot, own, first = fence((columns, crossing, pivot, own, first))
    right, own, first = fence((later_products(0), own, first))
    wide = col_pieces(own[SIB], first)
    wide, right = fence((wide, lax.psum(right, "col")))
    rights.append(right)
    columns.append(row_pieces(top_level(1)))
    rights.append(col_sum(later_products(1)))
    columns.append(row_pieces(top_level(2)))
    rights.append(col_sum(later_products(2)))
    columns.append(row_pieces(top_level(3)))
    columns, crossing, pivot = fence((columns, crossing, pivot))
    packed = call(
        functools.partial(pack_rows, levels),
        dims,
        sc,
        flat(columns),
        [blocks(levels)] * SIB,
        scratch=[pltpu.SemaphoreType.DMA((levels, SIB))],
        hbm=tuple(range(SIB * levels)),
    )
    rows = [packed[0]] + [swap(packed[s], "col", s) for s in range(1, SIB)]
    solved.append(row_pieces(window_level(0, 0, 0)[0]))
    (top_sum,) = call(
        functools.partial(cross_product, 3, levels), dims, sc, [*columns[3], *crossing], [blocks(1)], flops=4 * unit
    )
    top_sum = col_sum(top_sum)
    starts = [(0, 0, 0, True)]
    for k in range(1, levels - 1):
        if k == levels - 2:
            pivot, rows = fence((pivot, rows))
        solved.append(row_pieces(window_level(k, 0, k)[0]))
        starts.append((k, 0, SIB * k, True))
    k = levels - 1
    early, early_share = window_level(k, 0, k - 1)
    late, late_share = window_level(k, k - 1, k)
    (corner,) = call(
        functools.partial(pivot_block, k), dims, sc, [pivot, top_sum, early_share, late_share], [blocks(1)]
    )
    solved.append(row_pieces(early))
    starts.append((k, 0, SIB * (k - 1), False))
    solved.append(row_pieces(late))
    starts.append((k, k - 1, SIB, False))
    solved.append([swap(corner, "row", d) if d else corner for d in range(SIB)])
    starts.append((k, 0, 0, True))

    (out,) = call(
        functools.partial(place, starts),
        dims,
        sc,
        rows + flat(solved),
        [blocks(total // SIB, levels)],
    )
    return out[:, None, :, None]


def solution(mesh):
    in_specs = (
        P("pole", "row", None, "col", None, None),
        P("pole", "row", None, "col", None, None),
        P("pole", "row", None, None),
        P(),
        P(),
        P(),
    )
    out_specs = P("pole", "row", None, "col", None, None)
    square = mesh.shape["row"] == SIB and mesh.shape["col"] == SIB
    return jax.shard_map(
        square_plan if square else per_device, mesh=mesh, in_specs=in_specs, out_specs=out_specs, check_vma=False
    )
```

```python
import functools

import jax
import jax.numpy as jnp
from jax import lax
from jax.experimental import pallas as pl
from jax.experimental.pallas import tpu as pltpu
from jax.sharding import PartitionSpec as P

SIB = 4


def from_root(x, axis, root):
    mine = lax.axis_index(axis) == root
    return lax.psum(jnp.where(mine, x, jnp.zeros_like(x)), axis)


def per_device(top_inverse, upper_factor, pivot_inverse, widths, order, pattern):
    row_count = lax.axis_size("row")
    col_count = lax.axis_size("col")
    row_rank = lax.axis_index("row")
    col_rank = lax.axis_index("col")
    tile_size = top_inverse.shape[-1]
    total_nodes = widths.shape[0]
    window = order.shape[0]
    row_blocks = total_nodes // row_count
    col_blocks = total_nodes // col_count
    row_span = row_count // col_count
    factor = upper_factor[:, 0, :, 0]
    pivots = pivot_inverse[:, 0]
    live_rows = (
        lax.broadcasted_iota(jnp.int32, (total_nodes, tile_size), 1) < widths[:, None]
    ).astype(jnp.bfloat16)
    row_nodes = jnp.arange(row_blocks, dtype=jnp.int32) * row_count + row_rank
    col_nodes = jnp.arange(col_blocks, dtype=jnp.int32) * col_count + col_rank
    blocks_held = jnp.zeros((row_blocks, col_blocks, tile_size, tile_size), jnp.bfloat16)
    blocks_held = blocks_held.at[window // row_count :, window // col_count :].set(
        top_inverse[:, 0, :, 0]
    )
    members = SIB

    def fetch(node_id):
        local_rows = lax.dynamic_index_in_dim(factor, node_id // row_count, 0, keepdims=False)
        return from_root(local_rows, "row", node_id % row_count)

    def panel(node_id):
        received = fetch(node_id)
        present = pattern[col_nodes, node_id].astype(jnp.bfloat16)
        keep_mask = (
            present[:, None, None]
            * live_rows[col_nodes][:, None, :]
            * live_rows[node_id][None, :, None]
        )
        return received * keep_mask

    def step(position, blocks_held):
        node_ids = lax.dynamic_slice_in_dim(order, position * members, members)
        node_list = [node_ids[member] for member in range(members)]
        panels = jnp.stack([panel(node_id) for node_id in node_list])
        partial_value = jnp.einsum(
            "abpq,ibsq->iaps", blocks_held, panels, preferred_element_type=jnp.float32
        )
        summed = lax.psum_scatter(
            partial_value.astype(jnp.bfloat16), "col", scatter_dimension=2, tiled=True
        ).astype(jnp.float32)
        row_share = (-summed).astype(jnp.bfloat16)
        column_new = lax.all_gather(row_share, "col", axis=2, tiled=True)
        present = jnp.transpose(pattern[row_nodes][:, node_ids]).astype(jnp.bfloat16)
        node_live = live_rows[node_ids]
        column_mask = (
            present[:, :, None, None]
            * live_rows[row_nodes][None, :, :, None]
            * node_live[:, None, None, :]
        )
        column_new = column_new * column_mask
        for member, node_id in enumerate(node_list):
            column_at = node_id // col_count
            current = lax.dynamic_slice_in_dim(blocks_held, column_at, 1, 1)
            update = jnp.where(
                col_rank == node_id % col_count, column_new[member][:, None], current
            )
            blocks_held = lax.dynamic_update_slice_in_dim(blocks_held, update, column_at, 1)
        arrived = []
        for offset in range(row_span):
            arrived.append(from_root(column_new, "row", col_rank + offset * col_count))
        mirror = jnp.stack(arrived, 2).reshape(members, row_blocks * row_span, tile_size, tile_size)
        pivot_part = jnp.einsum(
            "ibsq,ibqt->ist", panels, mirror, preferred_element_type=jnp.float32
        )
        pivot_total = lax.psum(pivot_part.astype(jnp.bfloat16), "col").astype(jnp.float32)
        for member, node_id in enumerate(node_list):
            row_at = node_id // row_count
            column_at = node_id // col_count
            on_row = row_rank == node_id % row_count
            on_col = col_rank == node_id % col_count
            current = lax.dynamic_slice_in_dim(blocks_held, row_at, 1, 0)
            flipped = jnp.swapaxes(mirror[member], 1, 2)[None]
            update = jnp.where(on_row, flipped, current)
            own_pivot = lax.dynamic_index_in_dim(pivots, row_at, 0, keepdims=False)
            corner_mask = node_live[member][:, None].astype(jnp.float32) * node_live[member][
                None, :
            ].astype(jnp.float32)
            corner = ((own_pivot - pivot_total[member]) * corner_mask).astype(jnp.bfloat16)
            update = update.at[0, column_at].set(
                jnp.where(on_row & on_col, corner, update[0, column_at])
            )
            blocks_held = lax.dynamic_update_slice_in_dim(blocks_held, update, row_at, 0)
        return blocks_held

    blocks_held = lax.fori_loop(0, window // members, step, blocks_held)
    return blocks_held[:, : window // col_count][:, None, :, None]


VMEM_BYTES = 50 * 1024 * 1024
ORD = 2


def dot_nt(a, b):
    return lax.dot_general(a, b, (((1,), (1,)), ((), ())), preferred_element_type=jnp.float32)


def dot_nn(a, b):
    return jnp.dot(a, b, preferred_element_type=jnp.float32)


class Facts:
    def __init__(self, sc, window, total):
        self.sc, self.window = sc, window
        self.pat_at = ORD + window
        self.wid_at = self.pat_at + window * total
        self.r, self.c = sc[0], sc[1]

    def node(self, level, member):
        return self.sc[ORD + level * SIB + member]

    def pat(self, row, col):
        return self.sc[self.pat_at + row * self.window + col]

    def width(self, node):
        return self.sc[self.wid_at + node]


def keep(x, rows, cols):
    at_row = lax.broadcasted_iota(jnp.int32, x.shape, 0)
    at_col = lax.broadcasted_iota(jnp.int32, x.shape, 1)
    return jnp.where((at_row < rows) & (at_col < cols), x, 0.0)


def call(body, dims, sc, inputs, outs, scratch=(), hbm=(), flops=0):
    specs = [pl.BlockSpec(memory_space=pltpu.SMEM)]
    for at in range(len(inputs)):
        specs.append(pl.BlockSpec(memory_space=pl.ANY if at in hbm else pltpu.VMEM))
    moved = sum(x.size * x.dtype.itemsize for x in list(inputs) + list(outs))

    def kernel(sc_ref, *refs):
        body(Facts(sc_ref, *dims), *refs)

    return pl.pallas_call(
        kernel,
        out_shape=list(outs),
        in_specs=specs,
        out_specs=[pl.BlockSpec(memory_space=pltpu.VMEM)] * len(outs),
        scratch_shapes=list(scratch),
        compiler_params=pltpu.CompilerParams(vmem_limit_bytes=VMEM_BYTES),
        cost_estimate=pl.CostEstimate(flops=flops, bytes_accessed=moved, transcendentals=0),
    )(sc, *inputs)


def swap(x, axis, d):
    count = lax.axis_size(axis)
    return lax.ppermute(x, axis, [(i, i ^ d) for i in range(count)])


def row_pieces(x):
    far = swap(x, "row", 2)
    return [x, swap(x, "row", 1), far, swap(far, "row", 1)]


def col_hop(hop, down, up):
    last = SIB - 1
    return (
        lax.ppermute(down, "col", [(i + 1, i) for i in range(SIB - hop)]),
        lax.ppermute(up, "col", [(i, i + 1) for i in range(hop - 1, last)]),
    )


def col_pieces(x, first):
    rank = lax.axis_index("col")
    last = SIB - 1
    down, up = [x, first[0]], [x, first[1]]
    for hop in range(2, SIB):
        next_down, next_up = col_hop(hop, down[-1], up[-1])
        down.append(next_down)
        up.append(next_up)
    one = jnp.where(rank % 2 == 0, down[1], up[1])
    two = jnp.where(rank < 2, down[2], up[2])
    lower = jnp.where(rank == 0, down[3], down[1])
    upper = jnp.where(rank == last, up[3], up[1])
    return jnp.stack([x, one, two, jnp.where(rank < 2, lower, upper)])


def col_sum(x):
    last = SIB - 1
    at_end = (lax.axis_index("col") == 0) | (lax.axis_index("col") == last)

    def add(a, b):
        return (a.astype(jnp.float32) + b.astype(jnp.float32)).astype(jnp.bfloat16)

    half = add(x, lax.ppermute(x, "col", [(0, 1), (last, last - 1)]))
    full = add(half, lax.ppermute(half, "col", [(1, 2), (2, 1)]))
    return jnp.where(at_end, lax.ppermute(full, "col", [(1, 0), (last - 1, last)]), full)


def top_product(first, f, h, u0, u1, u2, u3, out, ubuf, lbuf, sems):
    pieces = (u0, u1, u2, u3)
    size = h.shape[-1]
    depth = h.shape[1]
    count = out.shape[1]
    for m in range(count):
        node = f.node(first, m)
        for d in range(SIB):

            @pl.when((node % SIB) ^ f.r == d)
            def _():
                pltpu.make_async_copy(pieces[d].at[node // SIB], ubuf.at[m], sems.at[m]).start()

    for m in range(count):
        node = f.node(first, m)
        pltpu.make_async_copy(u0.at[0], ubuf.at[m], sems.at[m]).wait()
        for b in range(depth):
            at = f.window + b * SIB + f.c
            reach = jnp.where(f.pat(at, node) > 0, f.width(at), 0)
            kept = keep(ubuf[m, b].astype(jnp.float32), size, reach)
            lbuf[m, :, b * size : (b + 1) * size] = kept.astype(jnp.bfloat16)
    for a in range(h.shape[0]):
        rows = jnp.concatenate([h[a, b] for b in range(depth)], axis=1)
        for m in range(count):
            out[a, m] = dot_nt(rows, lbuf[m]).astype(jnp.bfloat16)


def own_blocks(levels, f, *refs):
    tops, wins = refs[0:4], refs[4:8]
    by_slice, by_level, sems = refs[8:12], refs[12], refs[13]
    near = wins[0].shape[1]
    for wait in (False, True):
        for k in range(levels):
            node = f.node(k, f.r)
            at = node // SIB
            source = (node % SIB) ^ f.r
            for d in range(SIB):
                copies = [
                    pltpu.make_async_copy(tops[d].at[at, f.c ^ s], by_slice[s].at[k], sems.at[k, s])
                    for s in range(SIB)
                ]
                if k:
                    room = by_level.at[pl.ds((k - 1) * near, near)]
                    copies.append(pltpu.make_async_copy(wins[d].at[at], room, sems.at[k, SIB]))

                @pl.when(source == d)
                def _():
                    for copy in copies:
                        if wait:
                            copy.wait()
                        else:
                            copy.start()


def own_pivots(levels, f, p0, p1, p2, p3, out):
    pieces = (p0, p1, p2, p3)
    for k in range(levels):
        node = f.node(k, f.r)
        for d in range(SIB):

            @pl.when((node % SIB) ^ f.r == d)
            def _():
                out[k] = pieces[d][node // SIB]


def wide_at(level):
    return (level - 1) * SIB


def top_column(level, f, *refs):
    ys = refs[0:SIB]
    earlier = refs[SIB : SIB + SIB * level]
    out = refs[-1]
    node = f.node(level, f.r)
    acc = [y[...].astype(jnp.float32) for y in ys]
    if level:
        lw = refs[-2]
        for j in range(level):
            for d in range(SIB):
                at = f.node(j, f.r ^ d)
                block = lw[(at % SIB) ^ f.c, wide_at(level) + at // SIB]
                block = jnp.where(f.pat(at, node) > 0, block, jnp.zeros_like(block))
                for e in range(SIB):
                    acc[e] += dot_nt(earlier[j * SIB + d][d ^ e], block)
    for e in range(SIB):
        row = f.window + f.c * SIB + (f.r ^ e)
        reach = jnp.where(f.pat(row, node) > 0, f.width(row), 0)
        out[e] = keep(-acc[e], reach, f.width(node)).astype(jnp.bfloat16)


def cross_product(level, levels, f, *refs):
    xs, ts, out = refs[0:4], refs[4:8], refs[8]
    turn = f.c ^ f.r
    for k in range(level, levels):
        node = f.node(k, f.r)
        parts = []
        for s in range(SIB):
            row = f.window + f.c * SIB + (f.c ^ s)
            block = ts[s][k]
            parts.append(jnp.where(f.pat(row, node) > 0, block, jnp.zeros_like(block)))
        left = jnp.concatenate(parts, axis=1)
        for d in range(SIB if k > level else 1):
            right = jnp.concatenate([xs[d][turn ^ (s ^ d)] for s in range(SIB)], axis=0)
            at = (k - level - 1) * SIB + d if k > level else (levels - 1 - level) * SIB
            out[at] = dot_nn(left, right).astype(jnp.bfloat16)


def window_column(k, low, high, f, *refs):
    closing, carried = high == k, low > 0
    count = high - low + closing
    vs = refs[0:count]
    zs = [refs[count + SIB * i : count + SIB * (i + 1)] for i in range(k)]
    rest = list(refs[count + SIB * k :])
    node = f.node(k, f.r)
    width = f.width(node)
    if k:
        lw, ub = rest.pop(0), rest.pop()
    piv = rest.pop(0) if closing else None
    total = jnp.zeros(vs[0].shape[1:], jnp.float32)
    if carried:
        total += rest.pop(0)[0]
    out = rest.pop(0)
    for i in range(k):
        for d in range(SIB):
            at = f.node(i, f.r ^ d)
            block = lw[(at % SIB) ^ f.c, wide_at(k) + at // SIB]
            ub[i * SIB + d] = jnp.where(f.pat(at, node) > 0, block, jnp.zeros_like(block))
    for j in range(low, high):
        for d in range(SIB):
            acc = vs[j - low][(k - j - 1) * SIB + d].astype(jnp.float32)
            for i in range(k):
                for e in range(SIB):
                    left = ub[i * SIB + e]
                    if i > j:
                        acc += dot_nn(left, zs[i][e][j * SIB + (d ^ e)])
                    elif i < j:
                        acc += dot_nt(left, zs[j][d][i * SIB + (d ^ e)])
                    elif d == e:
                        acc += dot_nt(left, zs[j][d][j * SIB])
            at = f.node(j, f.r ^ d)
            reach = jnp.where(f.pat(at, node) > 0, f.width(at), 0)
            block = keep(-acc, width, reach).astype(jnp.bfloat16)
            out[(j - low) * SIB + d] = block
            total += dot_nt(ub[j * SIB + d], block)
    if closing:
        total += vs[-1][vs[-1].shape[0] - 1].astype(jnp.float32)
        corner = piv[k].astype(jnp.float32) - total
        out[(high - low) * SIB] = keep(corner, width, width).astype(jnp.bfloat16)
    else:
        rest[0][0] = total


def pack_rows(levels, f, *refs):
    xs, outs, sems = refs[: SIB * levels], refs[SIB * levels : SIB * levels + SIB], refs[-1]
    for wait in (False, True):
        for l in range(levels):
            for d in range(SIB):
                node = f.node(l, f.r ^ d)
                for s in range(SIB):

                    @pl.when((node % SIB) ^ f.c == s)
                    def _():
                        copy = pltpu.make_async_copy(
                            xs[l * SIB + d].at[d], outs[s].at[node // SIB], sems.at[l, d]
                        )
                        if wait:
                            copy.wait()
                        else:
                            copy.start()


def place(starts, f, *refs):
    rows, out = refs[0:SIB], refs[-1]
    top = out.shape[0] // 2
    for s in range(SIB):
        out[top + (f.c ^ s)] = rows[s][...]
    out[0:top] = jnp.zeros_like(out[0:top])
    for at, (k, low, count, corner) in enumerate(starts):
        for d in range(SIB):
            z = refs[SIB + at * SIB + d]
            node = f.node(k, f.r ^ d)
            on_row, on_col = node % SIB == f.r, node % SIB == f.c
            if count:

                @pl.loop(0, count)
                def _(at):
                    other = f.node(low + at // SIB, f.r ^ d ^ (at % SIB))

                    @pl.when(on_row & (other % SIB == f.c))
                    def _():
                        out[node // SIB, other // SIB] = z[at]

                    @pl.when(on_col & (other % SIB == f.r))
                    def _():
                        out[other // SIB, node // SIB] = z[at].T

            if corner:

                @pl.when(on_row & on_col)
                def _():
                    out[node // SIB, node // SIB] = z[count]


def square_plan(top_inverse, upper_factor, pivot_inverse, widths, order, pattern):
    row_rank = lax.axis_index("row")
    col_rank = lax.axis_index("col")
    size = top_inverse.shape[-1]
    total, window = widths.shape[0], order.shape[0]
    levels = window // SIB
    near = window // SIB
    bf16 = jnp.bfloat16
    dims = (window, total)

    def blocks(*lead, dtype=bf16):
        return jax.ShapeDtypeStruct((*lead, size, size), dtype)

    unit = 2 * size**3
    ranks = jnp.stack([row_rank, col_rank]).astype(jnp.int32)
    sc = jnp.concatenate([ranks, order, pattern.reshape(-1), widths])
    known = top_inverse[:, 0, :, 0]
    factor = upper_factor[:, 0, :, 0]
    tops = row_pieces(factor[:, near:])
    groups = [(0, 1), (1, levels - 1)]
    parts = [
        call(
            functools.partial(top_product, first),
            dims,
            sc,
            [known, *tops],
            [blocks(levels, SIB * count)],
            scratch=[
                pltpu.VMEM((SIB * count, levels, size, size), bf16),
                pltpu.VMEM((SIB * count, size, levels * size), bf16),
                pltpu.SemaphoreType.DMA((SIB * count,)),
            ],
            hbm=(1, 2, 3, 4),
            flops=64 * count * unit,
        )[0]
        for first, count in groups
    ]
    fence = lax.optimization_barrier
    sums = []
    for part, (_, count) in zip(parts, groups):
        total_part = lax.psum_scatter(part, "col", scatter_dimension=0)
        sums += [(total_part, at * SIB) for at in range(count)]
    window_factor, _ = fence((factor[:, :near], parts))
    wins = row_pieces(window_factor)
    own = call(
        functools.partial(own_blocks, levels),
        dims,
        sc,
        [*tops, *wins],
        [blocks(levels)] * SIB + [blocks((levels - 1) * near)],
        scratch=[pltpu.SemaphoreType.DMA((levels, SIB + 1))],
        hbm=tuple(range(8)),
    )
    own = list(own)

    def flat(lists):
        return [x for xs in lists for x in xs]

    def top_level(l):
        ys = []
        for d in range(SIB):
            share = lax.dynamic_index_in_dim(sums[l][0], sums[l][1] + (row_rank ^ d), 0, keepdims=False)
            ys.append(swap(share, "row", d) if d else share)
        return call(
            functools.partial(top_column, l),
            dims,
            sc,
            ys + flat(columns) + ([wide] if l else []),
            [blocks(SIB)],
            flops=16 * l * unit,
        )[0]

    def later_products(l):
        (right,) = call(
            functools.partial(cross_product, l, levels),
            dims,
            sc,
            [*columns[l], *crossing],
            [blocks(SIB * (levels - 1 - l) + 1)],
            flops=16 * (levels - 1 - l) * unit,
        )
        return right

    def window_level(k, low, high, share=None):
        closing = high == k
        outs = [blocks(SIB * (high - low) + closing)]
        inputs = rights[low : high + closing] + flat(solved)
        inputs += ([wide] if k else []) + ([pivot] if closing else [])
        if share is not None:
            inputs.append(share)
        if not closing:
            outs.append(blocks(1, dtype=jnp.float32))
        return call(
            functools.partial(window_column, k, low, high),
            dims,
            sc,
            inputs,
            outs,
            scratch=[pltpu.VMEM((SIB * k, size, size), bf16)] if k else [],
            flops=SIB * (high - low) * (SIB * k - 2) * unit,
        )

    columns, rights, solved = [], [], []
    crossing = [own[0]] + [swap(own[s], "col", s) for s in range(1, SIB)]
    first = col_hop(1, own[SIB], own[SIB])
    columns.append(row_pieces(top_level(0)))
    pivs = row_pieces(pivot_inverse[:, 0].astype(bf16))
    (pivot,) = call(functools.partial(own_pivots, levels), dims, sc, pivs, [blocks(levels)])
    columns, crossing, pivot, own, first = fence((columns, crossing, pivot, own, first))
    right, own, first = fence((later_products(0), own, first))
    wide = col_pieces(own[SIB], first)
    wide, right = fence((wide, lax.psum(right, "col")))
    rights.append(right)
    columns.append(row_pieces(top_level(1)))
    right, columns = fence((later_products(1), columns))
    rights.append(lax.psum(right, "col"))
    columns.append(row_pieces(top_level(2)))
    rights.append(col_sum(later_products(2)))
    columns.append(row_pieces(top_level(3)))
    columns, crossing, late_pivot = fence((columns, crossing, pivot))
    packed = call(
        functools.partial(pack_rows, levels),
        dims,
        sc,
        flat(columns),
        [blocks(levels)] * SIB,
        scratch=[pltpu.SemaphoreType.DMA((levels, SIB))],
        hbm=tuple(range(SIB * levels)),
    )
    rows = [packed[0]] + [swap(packed[s], "col", s) for s in range(1, SIB)]
    solved.append(row_pieces(window_level(0, 0, 0)[0]))
    (top_sum,) = call(
        functools.partial(cross_product, levels - 1, levels),
        dims,
        sc,
        [*columns[-1], *crossing],
        [blocks(1)],
        flops=4 * unit,
    )
    rights.append(col_sum(top_sum))
    starts = [(0, 0, 0, True)]
    pivot = late_pivot
    for k in range(1, levels - 1):
        solved.append(row_pieces(window_level(k, 0, k)[0]))
        starts.append((k, 0, SIB * k, True))
    k = levels - 1
    pivot, rows, rights[-1] = fence((pivot, rows, rights[-1]))
    early, share = window_level(k, 0, k - 1)
    (late,) = window_level(k, k - 1, k, share)
    solved.append(row_pieces(early))
    starts.append((k, 0, SIB * (k - 1), False))
    solved.append(row_pieces(late))
    starts.append((k, k - 1, SIB, True))

    (out,) = call(
        functools.partial(place, starts),
        dims,
        sc,
        rows + flat(solved),
        [blocks(total // SIB, levels)],
    )
    return out[:, None, :, None]


def solution(mesh):
    in_specs = (
        P("pole", "row", None, "col", None, None),
        P("pole", "row", None, "col", None, None),
        P("pole", "row", None, None),
        P(),
        P(),
        P(),
    )
    out_specs = P("pole", "row", None, "col", None, None)
    square = mesh.shape["row"] == SIB and mesh.shape["col"] == SIB
    return jax.shard_map(
        square_plan if square else per_device, mesh=mesh, in_specs=in_specs, out_specs=out_specs, check_vma=False
    )
```
